128 devices in a mesh: dp: 16 (over x, y), tensor: 8 (over z, core).
Axes of the slice: x: 4, y: 4, z: 4, core: 2. Of those that a mesh axis runs over, the one named last changes fastest.
Arguments:
- residual: bfloat16 [128, 7168], P(('dp', 'tensor')), may hold values from -6 to 6
- query_latent: bfloat16 [128, 64, 576], P(('dp', 'tensor')), may hold values from -16 to 16
- latent_cache: bfloat16 [128, 4096, 576], P(('dp', 'tensor')), may hold values from -5 to 5
- lengths: int32 [128], P(('dp', 'tensor')), may hold values from 2 to 4096
- w_uv: bfloat16 [64, 512, 128], P('tensor'), may hold values from -0.25 to 0.25
- w_o: bfloat16 [64, 128, 7168], P('tensor', 'dp'), may hold values from -1.75 to 1.75
- norm_gain: float32 [7168], replicated, may hold values from 0.1 to 1.9
- expert_ids: int32 [128, 8], P(('dp', 'tensor')), may hold values from 0 to 15, all different within a row; in each aligned block of 8 rows (0 to 7, 8 to 15, ...) at most 5 rows name the same one
- route_weights: float32 [128, 8], P(('dp', 'tensor')), may hold values from 0.1 to 0.6
- w_gate: bfloat16 [16, 7168, 2048], P('dp', None, 'tensor'), may hold values from -0.0625 to 0.0625
- w_up: bfloat16 [16, 7168, 2048], P('dp', None, 'tensor'), may hold values from -0.0625 to 0.0625
- w_down: bfloat16 [16, 2048, 7168], P('dp', 'tensor'), may hold values from -0.125 to 0.125
Outputs:
- layer_output: bfloat16 [128, 7168], P(('dp', 'tensor'))
The draws below stay inside these ranges and needn't reach their ends.
Inputs may be any that keep to these rules, and one draw needn't show every extreme that they name: `expert_ids`: each row names 8 different experts. Within the rows of one index of dp (aligned blocks of 8 rows) no expert is named by more than 5 rows, a bound that some block reaches.
All inputs are finite; a program needn't handle non-finite values.
Results may differ from the reference program's by a relative error of at most 0.0085.
Values may be sent and summed in bfloat16 or wider, within the bound.
A program may use at most 64 MiB of HBM per device.

```python
import math
import jax
import jax.numpy as jnp
import numpy as np
from jax import lax

D = 7168
H = 64
LAT = 512
ROPE = 64
HD = 128
FF = 2048
EXPERTS = 16
TOPK = 8
CTX = 4096
ROW_DEV = 1
ROWS = 128
CAP = 5
N_TENSOR = 8


def draw_latent_cache(key, part):
    key = jax.random.fold_in(key, 3)
    entries = jax.random.truncated_normal(key, -5.0, 5.0, (ROWS, CTX, LAT + ROPE), jnp.float32)
    return entries.astype(jnp.bfloat16)


def draw_query_latent(key, part):
    key = jax.random.fold_in(key, 5)
    entries = jax.random.truncated_normal(key, -5.0, 5.0, (ROWS, H, LAT + ROPE), jnp.float32)
    return entries.astype(jnp.bfloat16)


def draw_lengths(key, part):
    key = jax.random.fold_in(key, 7)
    subkeys = jax.random.split(key, 3)
    drawn_len = jax.random.randint(subkeys[0], (ROWS,), 2, CTX + 1)
    longest = jax.random.randint(subkeys[1], (), 0, ROWS)
    shortest = (longest + 1 + jax.random.randint(subkeys[2], (), 0, ROWS - 1)) % ROWS
    row_index = lax.iota(jnp.int32, ROWS)
    drawn_len = jnp.where(row_index == longest, CTX, drawn_len)
    return jnp.where(row_index == shortest, 2, drawn_len).astype(jnp.int32)


def block_scale(stream_key, extent, cuts, least, high):
    loudness, own = 1.0, jax.random.fold_in(stream_key, 6)
    for dim, blocks in cuts:
        heights = jnp.exp(jax.random.uniform(jax.random.fold_in(own, dim), (blocks,), jnp.float32, least / len(cuts), high / len(cuts)))
        loudness = loudness * jnp.repeat(heights, extent[dim] // blocks).reshape([-1 if axis == dim else 1 for axis in range(len(extent))])
    return loudness


def assign_block(stream_key, own, number, rows, number_of, top, reach, slope):
    ranking = jax.random.permutation(stream_key, number_of)
    crowded, common = shares(number_of, rows * top, reach, slope, True), shares(number_of, rows * top, reach, slope, False)
    places = jnp.arange(number_of)

    def named(sizes, rotation):
        used = int((sizes > 0).sum())
        fixed = max(1, used // 4)
        passed = fixed + (places - fixed + rotation * (used - fixed)) % max(1, number_of - fixed)
        return jnp.zeros((number_of,), jnp.int32).at[ranking[jnp.where(places < fixed, places, passed)]].set(jnp.asarray(sizes, jnp.int32))

    sizes = jnp.where(number % 4 == 0, named(crowded, number // 4), named(common, number - number // 4 - 1))
    mixed = jax.random.permutation(jax.random.fold_in(own, 3), number_of)
    donor, receiver = mixed[0:number_of // 2 * 2:2], mixed[1:number_of // 2 * 2:2]
    slack = jnp.minimum(sizes[donor] - 1, reach - sizes[receiver]) // 2
    slack = jnp.where((donor == ranking[0]) | (receiver == ranking[0]) | (sizes[receiver] == 0), 0, jnp.maximum(slack, 0))
    passed = jax.random.randint(jax.random.fold_in(own, 4), (number_of // 2,), 0, 1 << 20) % (slack + 1)
    sizes = sizes.at[donor].add(-passed).at[receiver].add(passed)
    items = jnp.searchsorted(jnp.cumsum(sizes), jnp.arange(rows * top), side="right").astype(jnp.int32)
    listing = items.reshape(top, rows).T
    listing = listing[jax.random.permutation(jax.random.fold_in(own, 1), rows)]
    rotation = jax.random.randint(jax.random.fold_in(own, 2), (rows, 1), 0, top)
    return jnp.take_along_axis(listing, (jnp.arange(top)[None, :] + rotation) % top, axis=1)


def shares(count, total, reach, lean, full):
    loads = [(1 << 20) // math.isqrt(grade ** lean) + 1 for grade in range(1, count + 1)]
    largest = reach if full else min(reach, max(-(-total // count), total * loads[0] // sum(loads)))
    least = 1 if total - largest >= count - 1 else 0
    holding, rest = [largest] + [least] * (count - 1), total - largest - least * (count - 1)
    while rest > 0:
        candidates = [i for i in range(1, count) if holding[i] < largest] or [i for i in range(1, count) if holding[i] < reach]
        whole, budget = sum([loads[i] for i in candidates]), rest
        for i in candidates:
            extra = min(reach - holding[i], max(1, budget * loads[i] // whole), rest)
            holding[i] = holding[i] + extra
            rest = rest - extra
    return np.array(holding)


def noise(key, extent, scale, bound, pieces=(), kind=jnp.bfloat16):
    loudness = block_scale(key, extent, pieces, -0.22, 0.18) if pieces else 1.0
    values = jax.random.normal(key, extent, jnp.float32) * scale * loudness
    return jnp.minimum(jnp.maximum(values, -bound), bound).astype(kind)


def setup_inputs(seed: int = 0) -> dict:
    seeds = jax.random.split(jax.random.key(seed), 13)
    residual = noise(seeds[0], (ROWS, D), 1.0, 6.0, ((0, 128),))
    query_latent = draw_query_latent(jax.random.fold_in(seeds[12], 71), 0)
    latent_cache = draw_latent_cache(jax.random.fold_in(seeds[12], 71), 0)
    lengths = draw_lengths(jax.random.fold_in(seeds[12], 71), 0)
    w_uv = noise(seeds[4], (H, LAT, HD), LAT ** -0.5, 0.25, ((0, 8),))
    w_o = noise(seeds[5], (H, HD, D), 0.12, 1.75, ((0, 8), (1, 16)))
    norm_gain = jnp.clip(1.0 + 0.18 * jax.random.normal(seeds[6], (D,), jnp.float32), 0.1, 1.9)
    expert_ids_keys = jax.random.split(jax.random.fold_in(seeds[7], 1), ROWS // (ROW_DEV * N_TENSOR))
    expert_ids_turns = jax.random.permutation(jax.random.fold_in(seeds[7], 3), ROWS // (ROW_DEV * N_TENSOR))
    expert_ids = jax.vmap(lambda own, number: assign_block(jax.random.fold_in(seeds[7], 2), own, number, ROW_DEV * N_TENSOR, EXPERTS, TOPK, CAP, 2))(expert_ids_keys, expert_ids_turns).reshape((ROWS, TOPK))
    route_weights = jnp.clip(0.1 + 0.5 * jax.random.uniform(seeds[8], (ROWS, TOPK), jnp.float32) ** block_scale(seeds[8], (ROWS, TOPK), ((0, 128),), -0.2, 0.2), 0.1, 0.6)
    w_gate = noise(seeds[9], (EXPERTS, D, FF), D ** -0.5, 0.0625, ((0, 16), (2, 8)))
    w_up = noise(seeds[10], (EXPERTS, D, FF), D ** -0.5, 0.0625, ((0, 16), (2, 8)))
    w_down = noise(seeds[11], (EXPERTS, FF, D), FF ** -0.5, 0.125, ((0, 16), (1, 8)))
    return dict(residual=residual, query_latent=query_latent, latent_cache=latent_cache, lengths=lengths, w_uv=w_uv, w_o=w_o, norm_gain=norm_gain, expert_ids=expert_ids, route_weights=route_weights, w_gate=w_gate, w_up=w_up, w_down=w_down)


masked_score = -1e+30
norm_eps = 1e-06

def attend_row(query_row, cache_row, length):
    score_scale = (HD + ROPE) ** (-0.5)
    scores = jnp.einsum('hc,pc->hp', query_row.astype(jnp.float32), cache_row.astype(jnp.float32)) * score_scale
    slot_index = jnp.arange(CTX, dtype=jnp.int32)
    active = (slot_index < length)[None, :]
    scores = jnp.where(active, scores, masked_score)
    row_max = lax.optimization_barrier(jnp.max(scores, axis=1, keepdims=True))
    weights = jnp.where(active, jnp.exp(scores - row_max), 0.0)
    totals = lax.optimization_barrier(jnp.sum(weights, axis=1))
    rounded = weights.astype(jnp.bfloat16)
    summed = jnp.einsum('hp,pc->hc', rounded.astype(jnp.float32), cache_row[:, :LAT].astype(jnp.float32))
    return (summed / totals[:, None]).astype(jnp.bfloat16)

def reference(residual, query_latent, latent_cache, lengths, w_uv, w_o, norm_gain, expert_ids, route_weights, w_gate, w_up, w_down):
    latent = lax.map(lambda items: attend_row(items[0], items[1], items[2]), (query_latent, latent_cache, lengths))
    values = jnp.einsum('rhc,hcv->rhv', latent.astype(jnp.float32), w_uv.astype(jnp.float32)).astype(jnp.bfloat16)
    attended = jnp.einsum('rhv,hvn->rn', values.astype(jnp.float32), w_o.astype(jnp.float32))
    stream = residual.astype(jnp.float32) + attended
    normed = (stream * lax.rsqrt(lax.optimization_barrier(jnp.mean(stream * stream, axis=1, keepdims=True)) + norm_eps) * norm_gain).astype(jnp.bfloat16)
    chosen = expert_ids[:, :, None] == jnp.arange(EXPERTS, dtype=jnp.int32)[None, None, :]
    coefficient = lax.optimization_barrier(jnp.sum(jnp.where(chosen, route_weights[:, :, None], 0.0), axis=1))

    def expert_pass(mixture, inputs):
        gate_weight, up_weight, down_weight, column = inputs
        gate_val = jnp.dot(normed, gate_weight, preferred_element_type=jnp.float32)
        up_val = jnp.dot(normed, up_weight, preferred_element_type=jnp.float32)
        activation = (jax.nn.silu(gate_val) * up_val).astype(jnp.bfloat16)
        expert_out = jnp.dot(activation, down_weight, preferred_element_type=jnp.float32)
        return (mixture + column[:, None] * expert_out, None)
    mixture, unused = lax.scan(expert_pass, jnp.zeros_like(stream), (w_gate, w_up, w_down, coefficient.T))
    return (stream + mixture).astype(jnp.bfloat16)
```

```python
import jax
import jax.numpy as jnp
from jax import lax
from jax.experimental import pallas as pl
from jax.experimental.pallas import tpu as pltpu
from jax.sharding import PartitionSpec as P

MESH = pl.DeviceIdType.MESH
F32 = jnp.float32
BF16 = jnp.bfloat16

CTX, CW, LAT = 4096, 576, 512
D, H, HD, FF = 7168, 64, 128, 256
CHUNK = 512
NCHUNK = CTX // CHUNK
WIN = 512
SCALE = 192 ** (-0.5)
EPS = 1e-06
MASKED = -1e30
PARTS = ((0, 2304), (2304, 2304), (4608, 2560))
ORDERS = (("z", "y", "x"), ("x", "z", "y"), ("y", "x", "z"))
TILE_ORDER = (0, 1, 2, 0)
SPAN = 24


def window_start(dp):
    return (dp // 2) * 896 + (dp % 2) * 384


def onehot(n, source):
    row = lax.broadcasted_iota(jnp.int32, (n, n), 0)
    col = lax.broadcasted_iota(jnp.int32, (n, n), 1)
    return jnp.where(col == source(row), 1.0, 0.0).astype(BF16)


def dot(a, b):
    return jnp.dot(a, b, preferred_element_type=F32)


def layer(
    len_ref, ids_ref, rw_ref, res_ref, q_ref, gain_ref,
    cache_hbm, wuv_hbm, wo_hbm, wg_hbm, wu_hbm, wd_hbm,
    out_ref,
    cache_v, wuv_v, wg_v, wu_v, wd_v,
    s_ref, resb_v, wo_recv, lat_send, lat_recv, vals_send, vals_all,
    rs_send, rs_recv, st_send, st_recv, x_v, ig2_v,
    d_own, c_send, c_recv, p1, p1r, q2f, q2, q2r, q3, q3r, mix_v,
    local_sem, a2a_s, a2a_r, rb_s, rb_r, lat_s, lat_r, val_s, val_r,
    rs_s, rs_r, st_s, st_r, ag_s, ag_r, sib_s, sib_r,
    cs_s, cs_r, p1_s, p1_r, p2_s, p2_r, p3_s, p3_r,
):
    dp = lax.axis_index("dp")
    t = lax.axis_index("tensor")
    pos = {"x": dp // 4, "y": dp % 4, "z": t // 2, "c": t % 2}
    core = pos["c"]

    def at_dp(i):
        return {"dp": lax.rem(dp + i, 16), "tensor": t}

    def at_t(i):
        return {"dp": dp, "tensor": lax.rem(t + i, 8)}

    def along(axis, i):
        new = dict(pos)
        new[axis] = lax.rem(pos[axis] + i, 4)
        return {"dp": new["x"] * 4 + new["y"], "tensor": new["z"] * 2 + new["c"]}

    sibling = {"dp": dp, "tensor": pos["z"] * 2 + (1 - core)}

    def remote(src, dst, ss, rs, dev):
        return pltpu.make_async_remote_copy(
            src_ref=src, dst_ref=dst, send_sem=ss, recv_sem=rs, device_id=dev, device_id_type=MESH
        )

    def each(n, f):
        def step(i, carry):
            f(i)
            return carry

        lax.fori_loop(1, n, step, 0)

    barrier = pltpu.get_barrier_semaphore()
    each(16, lambda i: pl.semaphore_signal(barrier, inc=1, device_id=at_dp(i), device_id_type=MESH))
    each(8, lambda i: pl.semaphore_signal(barrier, inc=1, device_id=at_t(i), device_id_type=MESH))

    def cache_copy(i):
        return pltpu.make_async_copy(
            cache_hbm.at[0, pl.ds(pl.multiple_of(i * CHUNK, CHUNK), CHUNK)],
            cache_v.at[i],
            local_sem.at[i],
        )

    def start_cache(i, carry):
        cache_copy(i).start()
        return carry

    lax.fori_loop(0, NCHUNK, start_cache, 0)

    start = pl.multiple_of(window_start(dp), 128)
    resb_v[...] = jnp.broadcast_to(res_ref[...].astype(F32), (8, D)).astype(BF16)
    own_wo = pltpu.make_async_copy(
        wo_hbm.at[:, :, pl.ds(start, WIN)], wo_recv.at[pl.ds(0, 8), dp], local_sem.at[NCHUNK]
    )
    own_wo.start()
    wo_recv[8, dp] = resb_v[:, pl.ds(start, WIN)]
    gain = gain_ref[...]
    ig2_v[...] = 1.0 / (gain * gain)

    pl.semaphore_wait(barrier, 22)

    def wo_copy(i):
        there = lax.rem(dp + i, 16)
        first = pl.multiple_of(window_start(there), 128)
        return remote(
            wo_hbm.at[:, :, pl.ds(first, WIN)], wo_recv.at[pl.ds(0, 8), dp],
            a2a_s.at[i], a2a_r.at[i], at_dp(i),
        )

    def res_copy(i):
        there = lax.rem(dp + i, 16)
        first = pl.multiple_of(window_start(there), 128)
        return remote(
            resb_v.at[:, pl.ds(first, WIN)], wo_recv.at[8, dp], rb_s.at[i], rb_r.at[i], at_dp(i)
        )

    each(16, lambda i: wo_copy(i).start())
    each(16, lambda i: res_copy(i).start())
    wuv_copy = pltpu.make_async_copy(wuv_hbm, wuv_v, local_sem.at[NCHUNK + 1])
    wuv_copy.start()

    length = len_ref[0]
    q = q_ref[0]

    def score(i, top):
        cache_copy(i).wait()
        s = lax.dot_general(
            q, cache_v[i], (((1,), (1,)), ((), ())), preferred_element_type=F32
        ) * SCALE
        slot = lax.broadcasted_iota(jnp.int32, (H, CHUNK), 1) + i * CHUNK
        s = jnp.where(slot < length, s, MASKED)
        s_ref[i] = s
        return jnp.maximum(top, jnp.max(s, axis=1, keepdims=True))

    top = lax.fori_loop(0, NCHUNK, score, jnp.full((H, 1), MASKED, F32))

    w_copies = [
        pltpu.make_async_copy(src, dst, local_sem.at[NCHUNK + 2 + k])
        for k, (src, dst) in enumerate(((wg_hbm, wg_v), (wu_hbm, wu_v), (wd_hbm, wd_v)))
    ]
    for copy in w_copies:
        copy.start()

    def mix(i, carry):
        total, acc = carry
        slot = lax.broadcasted_iota(jnp.int32, (H, CHUNK), 1) + i * CHUNK
        w = jnp.where(slot < length, jnp.exp(s_ref[i] - top), 0.0)
        total = total + jnp.sum(w, axis=1, keepdims=True)
        return total, acc + dot(w.astype(BF16), cache_v[i, :, :LAT])

    total, acc = lax.fori_loop(
        0, NCHUNK, mix, (jnp.zeros((H, 1), F32), jnp.zeros((H, LAT), F32))
    )
    latent = acc / total

    lane = lax.broadcasted_iota(jnp.int32, (1, 128), 1)
    coef = jnp.zeros((1, 128), F32)
    for k in range(8):
        coef = jnp.where(jnp.bitwise_and(lane, 15) == ids_ref[0, k], rw_ref[0, k], coef)
    high = coef.astype(BF16).astype(F32)
    coef = jnp.where(lane < 16, high, jnp.where(lane < 32, coef - high, 0.0))

    lat_send[:, :, :LAT] = latent.reshape(8, 8, LAT).astype(BF16)
    lat_send[:, :, LAT:] = jnp.broadcast_to(coef.reshape(1, 1, 128), (8, 8, 128)).astype(BF16)
    lat_recv[t] = lat_send[t]

    def lat_copy(i):
        return remote(
            lat_send.at[lax.rem(t + i, 8)], lat_recv.at[t], lat_s.at[i], lat_r.at[i], at_t(i)
        )

    def lat_wait(i):
        src = lax.rem(t - i + 8, 8)
        remote(lat_send.at[src], lat_recv.at[src], lat_s.at[i], lat_r.at[i], at_t(i)).wait_recv()

    each(8, lambda i: lat_copy(i).start())
    wuv_copy.wait()
    each(8, lat_wait)

    by_head = onehot(64, lambda r: jnp.bitwise_and(r, 7) * 8 + jnp.right_shift(r, 3))
    lat = lat_recv[...].astype(F32).reshape(64, LAT + 128).astype(BF16)
    lat = dot(by_head, lat)
    pieces = [dot(lat[8 * h : 8 * h + 8, :LAT].astype(BF16), wuv_v[h]) for h in range(8)]
    pieces.append(lat[0:8, LAT:])
    vals_send[...] = jnp.concatenate(pieces, axis=1).astype(BF16)
    vals_all[dp] = vals_send[...]

    def val_copy(i):
        return remote(vals_send, vals_all.at[dp], val_s.at[i], val_r.at[i], at_dp(i))

    def val_wait(i):
        src = lax.rem(dp - i + 16, 16)
        remote(vals_send, vals_all.at[src], val_s.at[i], val_r.at[i], at_dp(i)).wait_recv()

    each(16, lambda i: val_copy(i).start())

    def wo_wait(i):
        src = lax.rem(dp - i + 16, 16)
        remote(
            wo_hbm.at[:, :, pl.ds(start, WIN)], wo_recv.at[pl.ds(0, 8), src],
            a2a_s.at[i], a2a_r.at[i], at_dp(i),
        ).wait_recv()
        remote(
            resb_v.at[:, pl.ds(start, WIN)], wo_recv.at[8, src], rb_s.at[i], rb_r.at[i], at_dp(i)
        ).wait_recv()

    own_wo.wait()
    each(16, wo_wait)
    each(16, val_wait)

    to_t_order = onehot(128, lambda r: jnp.bitwise_and(r, 15) * 8 + jnp.right_shift(r, 4))
    vals = vals_all[...].astype(F32).reshape(128, 1152).astype(BF16)
    vals = dot(to_t_order, vals)
    row = lax.broadcasted_iota(jnp.int32, (128, 128), 0)
    col = lax.broadcasted_iota(jnp.int32, (128, 128), 1)
    pick = jnp.where(
        (jnp.right_shift(row, 4) == t) & (col == jnp.bitwise_and(row, 15) * 8), 1.0, 0.0
    ).astype(BF16)
    part = dot(pick, wo_recv[8].astype(F32).reshape(128, WIN).astype(BF16))
    for h in range(8):
        part = part + dot(
            vals[:, h * HD : (h + 1) * HD].astype(BF16),
            wo_recv[h].astype(F32).reshape(128, WIN).astype(BF16),
        )
    rs_send[...] = part.astype(BF16).reshape(8, 16, WIN)
    coefs = vals[:, 1024:]
    mine = (col == dp) | (col == dp + 16)
    coef_col = jnp.sum(jnp.where(mine, coefs, 0.0), axis=1, keepdims=True)

    def rs_copy(i):
        return remote(
            rs_send.at[lax.rem(t + i, 8)], rs_recv.at[t], rs_s.at[i], rs_r.at[i], at_t(i)
        )

    def rs_wait(i):
        src = lax.rem(t - i + 8, 8)
        remote(rs_send.at[src], rs_recv.at[src], rs_s.at[i], rs_r.at[i], at_t(i)).wait_recv()

    each(8, lambda i: rs_copy(i).start())
    rs_recv[t] = rs_send[t]
    each(8, rs_wait)
    stream = rs_recv[0].astype(F32)
    for k in range(1, 8):
        stream = stream + rs_recv[k].astype(F32)
    scaled = (stream * gain_ref[:, pl.ds(start, WIN)]).astype(BF16)
    for j in range(4):
        x_v[j, pos["x"], pos["y"], pos["z"], core] = scaled[:, 128 * j : 128 * j + 128]

    def block(j, free, fixed):
        at = dict(pos)
        at.update(fixed)
        index = [pl.ds(0, 4) if a in free else at[a] for a in ("x", "y", "z")]
        return x_v.at[j, index[0], index[1], index[2], at["c"]]

    def gather(j, phase, i):
        order = ORDERS[TILE_ORDER[j]]
        here = block(j, order[:phase], {})
        n = (j * 3 + phase) * 3 + i - 1
        return remote(here, here, ag_s.at[n], ag_r.at[n], along(order[phase], i))

    def gather_wait(j, phase, i):
        order = ORDERS[TILE_ORDER[j]]
        axis = order[phase]
        there = block(j, order[:phase], {axis: lax.rem(pos[axis] - i + 4, 4)})
        n = (j * 3 + phase) * 3 + i - 1
        remote(there, there, ag_s.at[n], ag_r.at[n], along(axis, i)).wait_recv()

    def to_sibling(j, i, c):
        order = ORDERS[TILE_ORDER[j]]
        axis = order[2]
        there = block(j, order[:2], {axis: lax.rem(pos[axis] - i + 4, 4), "c": c})
        return remote(there, there, sib_s.at[j * 4 + i], sib_r.at[j * 4 + i], sibling)

    for phase in range(3):
        for j in range(4):
            if phase:
                for i in (1, 2, 3):
                    gather_wait(j, phase - 1, i)
            for i in (2, 1, 3):
                gather(j, phase, i).start()
            if phase == 2:
                to_sibling(j, 0, core).start()

    st_send[...] = jnp.zeros_like(st_send)
    for j in range(4):
        st_send[pl.ds(j, 16, stride=8), :] = stream[:, 128 * j : 128 * j + 128]
    st_recv[dp] = st_send[pl.ds(pl.multiple_of(dp * 8, 8), 8), :]

    def st_copy(i):
        there = pl.multiple_of(lax.rem(dp + i, 16) * 8, 8)
        return remote(
            st_send.at[pl.ds(there, 8)], st_recv.at[dp], st_s.at[i], st_r.at[i], at_dp(i)
        )

    def st_wait(i):
        src = lax.rem(dp - i + 16, 16)
        remote(
            st_send.at[pl.ds(0, 8)], st_recv.at[src], st_s.at[i], st_r.at[i], at_dp(i)
        ).wait_recv()

    each(16, lambda i: st_copy(i).start())

    for i in (1, 3, 2):
        for j in range(4):
            gather_wait(j, 2, i)
            to_sibling(j, i, core).start()
    for i in (0, 1, 3, 2):
        for j in range(4):
            to_sibling(j, i, 1 - core).wait_recv()
    for copy in w_copies:
        copy.wait()

    def up_step(k, carry):
        g, u, sq = carry
        tiles = []
        for odd in range(2):
            for j in range(odd, 4):
                tiles.append(x_v[j, k // 2, 2 * lax.rem(k, 2) + odd].reshape(128, 128))
        for n, tile in enumerate(tiles):
            f = tile.astype(F32)
            sq = sq + f * f * ig2_v[:, pl.ds(pl.multiple_of(k * 896 + n * 128, 128), 128)]
        x = jnp.concatenate(tiles, axis=1)
        rows = pl.ds(pl.multiple_of(k * 896, 896), 896)
        return g + dot(x, wg_v[rows, :]), u + dot(x, wu_v[rows, :]), sq

    zero = jnp.zeros((128, FF), F32)
    g, u, sq = lax.fori_loop(0, 8, up_step, (zero, zero, jnp.zeros((128, 128), F32)))
    factor = lax.rsqrt(jnp.sum(sq, axis=1, keepdims=True) * (1.0 / D) + EPS)
    g = g * factor
    act = (g / (1.0 + jnp.exp(-g))) * (u * factor * coef_col)
    act = act.astype(BF16)

    bits = {"z": (5, 3), "c": (4, 1), "x": (2, 3), "y": (0, 3)}

    def core_copy(p):
        w = PARTS[p][1]
        return remote(
            c_send.at[p, :, pl.ds(0, w)], c_recv.at[p, :, pl.ds(0, w)], cs_s.at[p], cs_r.at[p], sibling
        )

    for p, (first, w) in enumerate(PARTS):
        order = ORDERS[p]

        def source(r):
            src = jnp.left_shift(jnp.bitwise_xor(jnp.right_shift(r, 6), core), 4)
            for a, shift in zip(order, (4, 2, 0)):
                src = src + jnp.left_shift(
                    jnp.bitwise_and(jnp.right_shift(r, shift), 3), bits[a][0]
                )
            return src

        act_p = dot(onehot(128, source), act).astype(BF16)

        def down(n, carry):
            o = dot(act_p, wd_v[:, pl.ds(pl.multiple_of(first + n * 256, 256), 256)])
            cols = pl.ds(pl.multiple_of(n * 256, 256), 256)
            d_own[p, :, cols] = o[:64]
            c_send[p, :, cols] = o[64:].astype(BF16)
            return carry

        lax.fori_loop(0, w // 256, down, 0)
        core_copy(p).start()

    def sum1(p, i):
        w = PARTS[p][1]
        axis = ORDERS[p][0]
        n = p * 3 + i - 1
        return remote(
            p1.at[p, lax.rem(pos[axis] + i, 4), :, pl.ds(0, w)], p1r.at[p, i - 1, :, pl.ds(0, w)],
            p1_s.at[n], p1_r.at[n], along(axis, i),
        )

    for p, (first, w) in enumerate(PARTS):
        core_copy(p).wait_recv()

        def pair(n, carry):
            cols = pl.ds(pl.multiple_of(n * 256, 256), 256)
            o = d_own[p, :, cols] + c_recv[p, :, cols].astype(F32)
            p1[p, :, :, cols] = o.reshape(4, 16, 256).astype(BF16)
            return carry

        lax.fori_loop(0, w // 256, pair, 0)
        for i in (2, 1, 3):
            sum1(p, i).start()

    def sum2(p, i):
        axis = ORDERS[p][1]
        n = p * 3 + i - 1
        return remote(
            q2.at[p, lax.rem(pos[axis] + i, 4)], q2r.at[p, i - 1], p2_s.at[n], p2_r.at[n], along(axis, i)
        )

    q2f[...] = jnp.zeros_like(q2f)
    for p, (first, w) in enumerate(PARTS):
        for i in (1, 3, 2):
            sum1(p, i).wait_recv()
        o = p1[p, pos[ORDERS[p][0]], :, 0:w].astype(F32)
        for i in range(3):
            o = o + p1r[p, i, :, 0:w].astype(F32)
        for j in range(w // 128):
            q2f[pl.ds(j, 16, stride=SPAN), :] = o[:, 128 * j : 128 * j + 128]
        q2[p] = q2f[...].astype(BF16).reshape(4, 4 * SPAN, 128)
        for i in (2, 1, 3):
            sum2(p, i).start()

    def sum3(p, i):
        axis = ORDERS[p][2]
        n = p * 3 + i - 1
        return remote(
            q3.at[p, lax.rem(pos[axis] + i, 4)], q3r.at[p, i - 1], p3_s.at[n], p3_r.at[n], along(axis, i)
        )

    for p in range(3):
        for i in (1, 3, 2):
            sum2(p, i).wait_recv()
        o = q2[p, pos[ORDERS[p][1]]].astype(F32)
        for i in range(3):
            o = o + q2r[p, i].astype(F32)
        q3[p] = o.reshape(4, SPAN, 128)
        for i in (2, 1, 3):
            sum3(p, i).start()

    each(16, st_wait)
    for k in range(8):
        mix_v[7 * k : 7 * k + 4, :] = st_recv[2 * k, 0:4, :]
        mix_v[7 * k + 4 : 7 * k + 7, :] = st_recv[2 * k + 1, 1:4, :]

    for p, (first, w) in enumerate(PARTS):
        for i in (1, 3, 2):
            sum3(p, i).wait_recv()
        o = q3[p, pos[ORDERS[p][2]]]
        for i in range(3):
            o = o + q3r[p, i]
        tiles = slice(first // 128, (first + w) // 128)
        mix_v[tiles, :] = mix_v[tiles, :] + o[: w // 128]
    out_ref[...] = mix_v[...].astype(BF16)

    each(16, lambda i: wo_copy(i).wait_send())
    each(16, lambda i: res_copy(i).wait_send())
    each(8, lambda i: lat_copy(i).wait_send())
    each(16, lambda i: val_copy(i).wait_send())
    each(8, lambda i: rs_copy(i).wait_send())
    each(16, lambda i: st_copy(i).wait_send())
    for j in range(4):
        for phase in range(3):
            for i in (1, 2, 3):
                gather(j, phase, i).wait_send()
        for i in range(4):
            to_sibling(j, i, core).wait_send()
    for p in range(3):
        core_copy(p).wait_send()
        for i in (1, 2, 3):
            sum1(p, i).wait_send()
            sum2(p, i).wait_send()
            sum3(p, i).wait_send()


def on_device(
    residual, query_latent, latent_cache, lengths, w_uv, w_o, norm_gain, expert_ids, route_weights,
    w_gate, w_up, w_down,
):
    dma = pltpu.SemaphoreType.DMA
    vmem = pl.BlockSpec(memory_space=pltpu.VMEM)
    smem = pl.BlockSpec(memory_space=pltpu.SMEM)
    hbm = pl.BlockSpec(memory_space=pl.ANY)
    wide = max(w for _, w in PARTS)
    out = pl.pallas_call(
        layer,
        out_shape=jax.ShapeDtypeStruct((D // 128, 128), BF16),
        in_specs=[smem, smem, smem, vmem, vmem, vmem] + [hbm] * 6,
        out_specs=vmem,
        scratch_shapes=[
            pltpu.VMEM((NCHUNK, CHUNK, CW), BF16),
            pltpu.VMEM((8, LAT, HD), BF16),
            pltpu.VMEM((D, FF), BF16),
            pltpu.VMEM((D, FF), BF16),
            pltpu.VMEM((FF, D), BF16),
            pltpu.VMEM((NCHUNK, H, CHUNK), F32),
            pltpu.VMEM((8, D), BF16),
            pltpu.VMEM((9, 16, 8, WIN), BF16),
            pltpu.VMEM((8, 8, LAT + 128), BF16),
            pltpu.VMEM((8, 8, LAT + 128), BF16),
            pltpu.VMEM((8, 1152), BF16),
            pltpu.VMEM((16, 8, 1152), BF16),
            pltpu.VMEM((8, 16, WIN), BF16),
            pltpu.VMEM((8, 16, WIN), BF16),
            pltpu.VMEM((128, 128), F32),
            pltpu.VMEM((16, 8, 128), F32),
            pltpu.VMEM((4, 4, 4, 4, 2, 16, 128), BF16),
            pltpu.VMEM((1, D), F32),
            pltpu.VMEM((3, 64, wide), F32),
            pltpu.VMEM((3, 64, wide), BF16),
            pltpu.VMEM((3, 64, wide), BF16),
            pltpu.VMEM((3, 4, 16, wide), BF16),
            pltpu.VMEM((3, 3, 16, wide), BF16),
            pltpu.VMEM((16 * SPAN, 128), F32),
            pltpu.VMEM((3, 4, 4 * SPAN, 128), BF16),
            pltpu.VMEM((3, 3, 4 * SPAN, 128), BF16),
            pltpu.VMEM((3, 4, SPAN, 128), F32),
            pltpu.VMEM((3, 3, SPAN, 128), F32),
            pltpu.VMEM((D // 128, 128), F32),
            dma((NCHUNK + 5,)),
            dma((16,)), dma((16,)), dma((16,)), dma((16,)),
            dma((8,)), dma((8,)), dma((16,)), dma((16,)),
            dma((8,)), dma((8,)), dma((16,)), dma((16,)),
            dma((36,)), dma((36,)), dma((16,)), dma((16,)),
            dma((3,)), dma((3,)), dma((9,)), dma((9,)), dma((9,)), dma((9,)), dma((9,)), dma((9,)),
        ],
        compiler_params=pltpu.CompilerParams(
            collective_id=0, has_side_effects=True, vmem_limit_bytes=56 * 1024 * 1024
        ),
    )(
        lengths, expert_ids, route_weights, residual, query_latent, norm_gain.reshape(1, D),
        latent_cache, w_uv, w_o, w_gate.reshape(D, FF), w_up.reshape(D, FF), w_down.reshape(FF, D),
    )
    return out.reshape(1, D)


def solution(mesh):
    return jax.shard_map(
        on_device,
        mesh=mesh,
        in_specs=(
            P(("dp", "tensor"), None),
            P(("dp", "tensor"), None, None),
            P(("dp", "tensor"), None, None),
            P(("dp", "tensor")),
            P("tensor", None, None),
            P("tensor", "dp", None),
            P(),
            P(("dp", "tensor"), None),
            P(("dp", "tensor"), None),
            P("dp", None, "tensor"),
            P("dp", None, "tensor"),
            P("dp", "tensor", None),
        ),
        out_specs=P(("dp", "tensor"), None),
        check_vma=False,
    )
```

```python
import jax
import jax.numpy as jnp
from jax import lax
from jax.experimental import pallas as pl
from jax.experimental.pallas import tpu as pltpu
from jax.sharding import PartitionSpec as P

MESH = pl.DeviceIdType.MESH
F32 = jnp.float32
BF16 = jnp.bfloat16

CTX, CW, LAT = 4096, 576, 512
D, H, HD, FF = 7168, 64, 128, 256
CHUNK = 1024
NCHUNK = CTX // CHUNK
WIN = 512
SCALE = 192 ** (-0.5)
EPS = 1e-06
MASKED = -1e30
PARTS = ((0, 2304), (2304, 2304), (4608, 2560))
PIECES = (
    (0, 0, 1280), (1, 0, 1280), (2, 0, 1280), (0, 1280, 1024), (1, 1280, 1024), (2, 1280, 1280),
)
ORDERS = (("z", "y", "x"), ("x", "z", "y"), ("y", "x", "z"))
TILE_ORDER = ((0, 1, 2, 0), (1, 2, 0, 1))
SPAN = 24
PLANE = (
    (2, 2), (2, 1), (1, 2), (2, 3), (3, 2), (2, 0), (0, 2), (1, 1), (3, 3), (1, 3), (3, 1),
    (1, 0), (0, 1), (3, 0), (0, 3),
)
LINE = ((2, 1), (2, 0), (1, 1), (3, 1), (1, 0), (3, 0), (0, 1))


def window_start(dp):
    return (dp // 2) * 896 + (dp % 2) * 384


def onehot(n, source):
    row = lax.broadcasted_iota(jnp.int32, (n, n), 0)
    col = lax.broadcasted_iota(jnp.int32, (n, n), 1)
    return jnp.where(col == source(row), 1.0, 0.0).astype(BF16)


def dot(a, b):
    return jnp.dot(a, b, preferred_element_type=F32)


def layer(
    len_hbm, ids_hbm, rw_hbm, res_hbm, q_hbm, gain_hbm,
    cache_hbm, wuv_hbm, wo_hbm, wg_hbm, wu_hbm, wd_hbm,
    out_ref,
    len_ref, ids_ref, rw_ref, res_ref, q_ref, gain_ref,
    cache_v, wuv_v, wg_v, wu_v, wd_v,
    s_ref, resf_v, res_recv, wo_recv, lat_send, lat_recv, vals_send, vals_all,
    rs_send, rs_recv, st_send, st_recv, x_v, ig2_v,
    d_own, c_send, c_recv, p1, p1r, q2f, q2, q2r, q3, q3r, mix_v,
    local_sem, a2a_s, a2a_r, rb_s, rb_r, lat_s, lat_r, val_s, val_r,
    rs_s, rs_r, st_s, st_r, ag_s, ag_r, sib_s, sib_r,
    cs_s, cs_r, p1_s, p1_r, p2_s, p2_r, p3_s, p3_r,
):
    dp = lax.axis_index("dp")
    t = lax.axis_index("tensor")
    pos = {"x": dp // 4, "y": dp % 4, "z": t // 2, "c": t % 2}
    core = pos["c"]

    def dp_of(step):
        return lax.rem(pos["x"] + step[0], 4) * 4 + lax.rem(pos["y"] + step[1], 4)

    def dp_before(step):
        return lax.rem(pos["x"] + 4 - step[0], 4) * 4 + lax.rem(pos["y"] + 4 - step[1], 4)

    def t_of(step):
        return lax.rem(pos["z"] + step[0], 4) * 2 + lax.rem(core + step[1], 2)

    def t_before(step):
        return lax.rem(pos["z"] + 4 - step[0], 4) * 2 + lax.rem(core + step[1], 2)

    def at_dp(step):
        return {"dp": dp_of(step), "tensor": t}

    def at_t(step):
        return {"dp": dp, "tensor": t_of(step)}

    def along(axis, i):
        new = dict(pos)
        new[axis] = lax.rem(pos[axis] + i, 4)
        return {"dp": new["x"] * 4 + new["y"], "tensor": new["z"] * 2 + new["c"]}

    sibling = {"dp": dp, "tensor": pos["z"] * 2 + (1 - core)}

    def remote(src, dst, ss, rs, dev):
        return pltpu.make_async_remote_copy(
            src_ref=src, dst_ref=dst, send_sem=ss, recv_sem=rs, device_id=dev, device_id_type=MESH
        )

    def each(n, f):
        def step(i, carry):
            f(i)
            return carry

        lax.fori_loop(0, n, step, 0)

    barrier = pltpu.get_barrier_semaphore()
    for step in PLANE:
        pl.semaphore_signal(barrier, inc=1, device_id=at_dp(step), device_id_type=MESH)
    for step in LINE:
        pl.semaphore_signal(barrier, inc=1, device_id=at_t(step), device_id_type=MESH)

    def cache_copy(i):
        return pltpu.make_async_copy(
            cache_hbm.at[0, :, pl.ds(pl.multiple_of(i * CHUNK, CHUNK), CHUNK)],
            cache_v.at[i],
            local_sem.at[i],
        )

    def local(n, src, dst):
        return pltpu.make_async_copy(src, dst, local_sem.at[NCHUNK + n])

    small = [
        local(0, q_hbm.at[0], q_ref), local(1, len_hbm, len_ref), local(2, res_hbm, res_ref),
        local(3, gain_hbm, gain_ref), local(4, ids_hbm, ids_ref), local(5, rw_hbm, rw_ref),
    ]
    small[0].start()
    small[1].start()
    cache_copy(0).start()
    small[2].start()
    for i in range(1, NCHUNK):
        cache_copy(i).start()
    for copy in small[3:]:
        copy.start()
    start = pl.multiple_of(window_start(dp), 128)
    own_wo = local(6, wo_hbm.at[:, :, pl.ds(start, WIN)], wo_recv.at[:, dp])
    own_wo.start()
    wuv_copy = local(7, wuv_hbm, wuv_v)
    wuv_copy.start()

    for copy in small[:2]:
        copy.wait()
    length = len_ref[0]
    q = q_ref[...]

    def score(i, top):
        cache_copy(i).wait()
        s = dot(q, cache_v[i]) * SCALE
        slot = lax.broadcasted_iota(jnp.int32, (H, CHUNK), 1) + i * CHUNK
        s = jnp.where(slot < length, s, MASKED)
        s_ref[i] = s
        return jnp.maximum(top, jnp.max(s, axis=1, keepdims=True))

    top = jnp.full((H, 1), MASKED, F32)
    for i in range(NCHUNK // 2):
        top = score(i, top)

    small[2].wait()
    resf_v[...] = res_ref[...].astype(F32)
    pl.semaphore_wait(barrier, 22)

    def wo_copy(n, src_dp, slot, skip):
        first = pl.multiple_of(window_start(src_dp) + skip, 128)
        return remote(
            wo_hbm.at[:, :, pl.ds(first, WIN - skip)],
            wo_recv.at[:, slot, :, pl.ds(skip, WIN - skip)],
            a2a_s.at[n], a2a_r.at[n], at_dp(PLANE[n]),
        )

    def by_parity(odd, f):
        pl.when(odd == 0)(lambda: f(0))
        pl.when(odd == 1)(lambda: f(128))

    def res_copy(n):
        first = pl.multiple_of(window_start(dp_of(PLANE[n])), 128)
        return remote(
            resf_v.at[:, pl.ds(first, WIN)], res_recv.at[dp],
            rb_s.at[n], rb_r.at[n], at_dp(PLANE[n]),
        )

    for n, step in enumerate(PLANE):
        by_parity(
            lax.rem(dp_of(step), 2),
            lambda skip, n=n, step=step: wo_copy(n, dp_of(step), dp, skip).start(),
        )
    res_recv[dp] = resf_v[:, pl.ds(start, WIN)]
    for n in range(15):
        res_copy(n).start()

    for i in range(NCHUNK // 2, NCHUNK):
        top = score(i, top)

    w_copies = [local(8 + k, src, dst) for k, (src, dst) in enumerate(
        ((wg_hbm, wg_v), (wu_hbm, wu_v), (wd_hbm, wd_v)))]
    for copy in w_copies:
        copy.start()

    total = jnp.zeros((H, 1), F32)
    acc = jnp.zeros((H, LAT), F32)
    for i in range(NCHUNK):
        slot = lax.broadcasted_iota(jnp.int32, (H, CHUNK), 1) + i * CHUNK
        w = jnp.where(slot < length, jnp.exp(s_ref[i] - top), 0.0)
        total = total + jnp.sum(w, axis=1, keepdims=True)
        acc = acc + lax.dot_general(
            w.astype(BF16), cache_v[i, :LAT], (((1,), (1,)), ((), ())), preferred_element_type=F32
        )
    latent = acc / total

    for copy in small[4:]:
        copy.wait()
    lane = lax.broadcasted_iota(jnp.int32, (1, 128), 1)
    coef = jnp.zeros((1, 128), F32)
    for k in range(8):
        coef = jnp.where(jnp.bitwise_and(lane, 15) == ids_ref[0, k], rw_ref[0, k], coef)
    high = coef.astype(BF16).astype(F32)
    coef = jnp.where(lane < 16, high, jnp.where(lane < 32, coef - high, 0.0))

    lat_send[:, :, :LAT] = latent.reshape(8, 8, LAT).astype(BF16)
    lat_send[:, :, LAT:] = jnp.broadcast_to(coef.reshape(1, 1, 128), (8, 8, 128)).astype(BF16)

    def lat_copy(n):
        return remote(
            lat_send.at[t_of(LINE[n])], lat_recv.at[t], lat_s.at[n], lat_r.at[n], at_t(LINE[n])
        )

    def lat_wait(n):
        src = t_before(LINE[n])
        remote(lat_send.at[src], lat_recv.at[src], lat_s.at[n], lat_r.at[n], at_t(LINE[n])).wait_recv()

    for n in range(7):
        lat_copy(n).start()
    lat_recv[t] = lat_send[t]
    small[3].wait()
    gain = gain_ref[...]
    ig2_v[...] = 1.0 / (gain * gain)
    wuv_copy.wait()
    for n in range(7):
        lat_wait(n)

    by_head = onehot(64, lambda r: jnp.bitwise_and(r, 7) * 8 + jnp.right_shift(r, 3))
    lat = lat_recv[...].astype(F32).reshape(64, LAT + 128).astype(BF16)
    lat = dot(by_head, lat)
    pieces = [dot(lat[8 * h : 8 * h + 8, :LAT].astype(BF16), wuv_v[h]) for h in range(8)]
    pieces.append(lat[0:8, LAT:])
    vals_send[...] = jnp.concatenate(pieces, axis=1).astype(BF16)

    def val_copy(n):
        return remote(vals_send, vals_all.at[dp], val_s.at[n], val_r.at[n], at_dp(PLANE[n]))

    def val_wait(n):
        src = dp_before(PLANE[n])
        remote(vals_send, vals_all.at[src], val_s.at[n], val_r.at[n], at_dp(PLANE[n])).wait_recv()

    for n in range(15):
        val_copy(n).start()
    vals_all[dp] = vals_send[...]
    own_wo.wait()
    for n in range(15):
        by_parity(
            lax.rem(dp, 2),
            lambda skip, n=n: wo_copy(n, dp, dp_before(PLANE[n]), skip).wait_recv(),
        )
    for n in range(15):
        val_wait(n)

    to_t_order = onehot(128, lambda r: jnp.bitwise_and(r, 15) * 8 + jnp.right_shift(r, 4))
    vals_raw = vals_all[...].astype(F32).reshape(128, 1152).astype(BF16)
    vals = dot(to_t_order, vals_raw[:, : 8 * HD]).astype(BF16)
    part = jnp.zeros((128, WIN), F32)
    for h in range(8):
        part = part + dot(
            vals[:, h * HD : (h + 1) * HD], wo_recv[h].astype(F32).reshape(128, WIN).astype(BF16)
        )
    rs_send[...] = part.astype(BF16).reshape(8, 16, WIN)

    def rs_copy(n):
        return remote(
            rs_send.at[t_of(LINE[n])], rs_recv.at[t], rs_s.at[n], rs_r.at[n], at_t(LINE[n])
        )

    def rs_wait(n):
        src = t_before(LINE[n])
        remote(rs_send.at[src], rs_recv.at[src], rs_s.at[n], rs_r.at[n], at_t(LINE[n])).wait_recv()

    for n in range(7):
        rs_copy(n).start()
    rs_recv[t] = rs_send[t]

    to_c_order = onehot(
        128,
        lambda r: jnp.bitwise_and(r, 15) * 8
        + jnp.bitwise_and(jnp.right_shift(r, 4), 3) * 2
        + jnp.right_shift(r, 6),
    )
    coefs = dot(to_c_order, vals_raw[:, 8 * HD :])
    col = lax.broadcasted_iota(jnp.int32, (128, 128), 1)
    mine = (col == dp) | (col == dp + 16)
    coef_col = jnp.sum(jnp.where(mine, coefs, 0.0), axis=1, keepdims=True)

    for n in range(15):
        src = dp_before(PLANE[n])
        remote(
            resf_v.at[:, pl.ds(start, WIN)], res_recv.at[src],
            rb_s.at[n], rb_r.at[n], at_dp(PLANE[n]),
        ).wait_recv()
    res = jnp.concatenate([res_recv[k] for k in range(16)], axis=0)

    for n in range(7):
        rs_wait(n)
    stream = res
    for k in range(8):
        stream = stream + rs_recv[k].astype(F32)
    scaled = (stream * gain_ref[:, pl.ds(start, WIN)]).astype(BF16)

    def either(c, f):
        zero, one = f(0), f(1)
        return zero + c * (one - zero)

    def axis_of(j, c, k):
        return ORDERS[TILE_ORDER[c][j]][k]

    def place(j, k, c):
        return either(c, lambda v: pos[axis_of(j, v, k)])

    def block(j, phase, c, i):
        at = [place(j, k, c) for k in (2, 1, 0)][: 3 - phase]
        at[-1] = lax.rem(at[-1] - i + 4, 4)
        return x_v.at[(j, c, *at)]

    def partner(j, k, i):
        return {
            name: either(core, lambda v, name=name: along(axis_of(j, v, k), i)[name])
            for name in ("dp", "tensor")
        }

    def gather(j, phase, i):
        here = block(j, phase, core, 0)
        n = (j * 3 + phase) * 3 + i - 1
        return remote(here, here, ag_s.at[n], ag_r.at[n], partner(j, phase, i))

    def gather_wait(j, phase, i):
        there = block(j, phase, core, i)
        n = (j * 3 + phase) * 3 + i - 1
        remote(there, there, ag_s.at[n], ag_r.at[n], partner(j, phase, i)).wait_recv()

    def to_sibling(j, i, c):
        there = block(j, 2, c, i)
        return remote(there, there, sib_s.at[j * 4 + i], sib_r.at[j * 4 + i], sibling)

    for j in range(4):
        x_v[j, core, place(j, 2, core), place(j, 1, core), place(j, 0, core)] = scaled[
            :, 128 * j : 128 * j + 128
        ]
        for i in (2, 1, 3):
            gather(j, 0, i).start()

    st_send[...] = jnp.zeros_like(st_send)
    for j in range(4):
        st_send[pl.ds(j, 16, stride=8), :] = stream[:, 128 * j : 128 * j + 128]
    st_recv[dp] = st_send[pl.ds(pl.multiple_of(dp * 8, 8), 8), :]

    def st_copy(n):
        there = pl.multiple_of(dp_of(PLANE[n]) * 8, 8)
        return remote(
            st_send.at[pl.ds(there, 8)], st_recv.at[dp], st_s.at[n], st_r.at[n], at_dp(PLANE[n])
        )

    def st_wait(n):
        src = dp_before(PLANE[n])
        remote(
            st_send.at[pl.ds(0, 8)], st_recv.at[src], st_s.at[n], st_r.at[n], at_dp(PLANE[n])
        ).wait_recv()

    for phase in (1, 2):
        for j in range(4):
            for i in (1, 3, 2):
                gather_wait(j, phase - 1, i)
            for i in (2, 1, 3):
                gather(j, phase, i).start()
            if phase == 2:
                to_sibling(j, 0, core).start()

    for n in range(15):
        st_copy(n).start()
    for n in range(15):
        by_parity(
            lax.rem(dp_of(PLANE[n]), 2),
            lambda skip, n=n: wo_copy(n, dp_of(PLANE[n]), dp, skip).wait_send(),
        )
        res_copy(n).wait_send()
        val_copy(n).wait_send()
    for n in range(7):
        lat_copy(n).wait_send()
        rs_copy(n).wait_send()

    for i in (1, 3, 2):
        for j in range(4):
            gather_wait(j, 2, i)
            to_sibling(j, i, core).start()
    for i in (0, 1, 3, 2):
        for j in range(4):
            to_sibling(j, i, 1 - core).wait_recv()
    for copy in w_copies:
        copy.wait()

    def tile_of(j, x, y):
        halves = []
        for c in range(2):
            at = {"x": x, "y": y, "z": slice(None)}
            i1, i2, i3 = (at[a] for a in ORDERS[TILE_ORDER[c][j]])
            halves.append(x_v[j, c, i3, i2, i1].reshape(64, 128))
        return jnp.concatenate(halves, axis=0)

    def up_step(k, carry):
        g, u, sq = carry
        tiles = []
        for odd in range(2):
            for j in range(odd, 4):
                tiles.append(tile_of(j, k // 2, 2 * lax.rem(k, 2) + odd))
        for n, tile in enumerate(tiles):
            f = tile.astype(F32)
            sq = sq + f * f * ig2_v[:, pl.ds(pl.multiple_of(k * 896 + n * 128, 128), 128)]
        x = jnp.concatenate(tiles, axis=1)
        rows = pl.ds(pl.multiple_of(k * 896, 896), 896)
        return g + dot(x, wg_v[rows, :]), u + dot(x, wu_v[rows, :]), sq

    zero = jnp.zeros((128, FF), F32)
    g, u, sq = lax.fori_loop(0, 8, up_step, (zero, zero, jnp.zeros((128, 128), F32)))
    factor = lax.rsqrt(jnp.sum(sq, axis=1, keepdims=True) * (1.0 / D) + EPS)
    g = g * factor
    act = (g / (1.0 + jnp.exp(-g))) * (u * factor * coef_col)
    act = act.astype(BF16)

    bits = {"c": 6, "z": 4, "x": 2, "y": 0}
    acts = []
    for p in range(3):

        def source(r):
            src = jnp.left_shift(jnp.bitwise_xor(jnp.right_shift(r, 6), core), bits["c"])
            for a, shift in zip(ORDERS[p], (4, 2, 0)):
                src = src + jnp.left_shift(jnp.bitwise_and(jnp.right_shift(r, shift), 3), bits[a])
            return src

        acts.append(dot(onehot(128, source), act).astype(BF16))

    def core_copy(s):
        p, at, w = PIECES[s]
        cols = pl.ds(at, w)
        return remote(
            c_send.at[p, :, cols], c_recv.at[p, :, cols], cs_s.at[s], cs_r.at[s], sibling
        )

    def sum1(s, i):
        p, at, w = PIECES[s]
        axis = ORDERS[p][0]
        n = s * 3 + i - 1
        cols = pl.ds(at, w)
        return remote(
            p1.at[p, lax.rem(pos[axis] + i, 4), :, cols], p1r.at[p, i - 1, :, cols],
            p1_s.at[n], p1_r.at[n], along(axis, i),
        )

    def down(s):
        p, at, w = PIECES[s]
        first = PARTS[p][0] + at
        o = dot(acts[p], wd_v[:, first : first + w])
        d_own[p, :, at : at + w] = o[:64]
        c_send[p, :, at : at + w] = o[64:].astype(BF16)
        core_copy(s).start()

    def pair(s):
        p, at, w = PIECES[s]
        core_copy(s).wait_recv()
        o = d_own[p, :, at : at + w] + c_recv[p, :, at : at + w].astype(F32)
        p1[p, :, :, at : at + w] = o.reshape(4, 16, w).astype(BF16)
        for i in (2, 1, 3):
            sum1(s, i).start()

    down(0)
    for s in range(1, 6):
        down(s)
        pair(s - 1)
    pair(5)

    def sum2(p, i):
        axis = ORDERS[p][1]
        n = p * 3 + i - 1
        return remote(
            q2.at[p, lax.rem(pos[axis] + i, 4)], q2r.at[p, i - 1], p2_s.at[n], p2_r.at[n], along(axis, i)
        )

    q2f[...] = jnp.zeros_like(q2f)
    for p, (first, w) in enumerate(PARTS):
        for s in (p, p + 3):
            for i in (1, 3, 2):
                sum1(s, i).wait_recv()
        o = p1[p, pos[ORDERS[p][0]], :, 0:w].astype(F32)
        for i in range(3):
            o = o + p1r[p, i, :, 0:w].astype(F32)
        for j in range(w // 128):
            q2f[pl.ds(j, 16, stride=SPAN), :] = o[:, 128 * j : 128 * j + 128]
        q2[p] = q2f[...].astype(BF16).reshape(4, 4 * SPAN, 128)
        for i in (2, 1, 3):
            sum2(p, i).start()

    def sum3(p, i):
        axis = ORDERS[p][2]
        n = p * 3 + i - 1
        return remote(
            q3.at[p, lax.rem(pos[axis] + i, 4)], q3r.at[p, i - 1], p3_s.at[n], p3_r.at[n], along(axis, i)
        )

    for n in range(15):
        st_wait(n)
        st_copy(n).wait_send()
    for k in range(8):
        mix_v[7 * k : 7 * k + 4, :] = st_recv[2 * k, 0:4, :]
        mix_v[7 * k + 4 : 7 * k + 7, :] = st_recv[2 * k + 1, 1:4, :]

    for p in range(3):
        for i in (1, 3, 2):
            sum2(p, i).wait_recv()
        o = q2[p, pos[ORDERS[p][1]]].astype(F32)
        for i in range(3):
            o = o + q2r[p, i].astype(F32)
        q3[p] = o.reshape(4, SPAN, 128)
        for i in (2, 1, 3):
            sum3(p, i).start()

    for j in range(4):
        for phase in range(3):
            for i in (1, 2, 3):
                gather(j, phase, i).wait_send()
        for i in range(4):
            to_sibling(j, i, core).wait_send()
    for s in range(6):
        core_copy(s).wait_send()
        for i in (1, 2, 3):
            sum1(s, i).wait_send()
    for p in range(3):
        for i in (1, 2, 3):
            sum2(p, i).wait_send()

    for p, (first, w) in enumerate(PARTS):
        for i in (1, 3, 2):
            sum3(p, i).wait_recv()
        o = q3[p, pos[ORDERS[p][2]]]
        for i in range(3):
            o = o + q3r[p, i]
        tiles = slice(first // 128, (first + w) // 128)
        mix_v[tiles, :] = mix_v[tiles, :] + o[: w // 128]
    out_ref[...] = mix_v[...].astype(BF16)
    for p in range(3):
        for i in (1, 2, 3):
            sum3(p, i).wait_send()


def on_device(
    residual, query_latent, latent_cache, lengths, w_uv, w_o, norm_gain, expert_ids, route_weights,
    w_gate, w_up, w_down,
):
    dma = pltpu.SemaphoreType.DMA
    vmem = pl.BlockSpec(memory_space=pltpu.VMEM)
    hbm = pl.BlockSpec(memory_space=pl.ANY)
    wide = max(w for _, w in PARTS)
    out = pl.pallas_call(
        layer,
        out_shape=jax.ShapeDtypeStruct((D // 128, 128), BF16),
        in_specs=[hbm] * 12,
        out_specs=vmem,
        scratch_shapes=[
            pltpu.SMEM((1,), jnp.int32),
            pltpu.SMEM((1, 8), jnp.int32),
            pltpu.SMEM((1, 8), F32),
            pltpu.VMEM((1, D), BF16),
            pltpu.VMEM((H, CW), BF16),
            pltpu.VMEM((1, D), F32),
            pltpu.VMEM((NCHUNK, CW, CHUNK), BF16),
            pltpu.VMEM((8, LAT, HD), BF16),
            pltpu.VMEM((D, FF), BF16),
            pltpu.VMEM((D, FF), BF16),
            pltpu.VMEM((FF, D), BF16),
            pltpu.VMEM((NCHUNK, H, CHUNK), F32),
            pltpu.VMEM((1, D), F32),
            pltpu.VMEM((16, 1, WIN), F32),
            pltpu.VMEM((8, 16, 8, WIN), BF16),
            pltpu.VMEM((8, 8, LAT + 128), BF16),
            pltpu.VMEM((8, 8, LAT + 128), BF16),
            pltpu.VMEM((8, 1152), BF16),
            pltpu.VMEM((16, 8, 1152), BF16),
            pltpu.VMEM((8, 16, WIN), BF16),
            pltpu.VMEM((8, 16, WIN), BF16),
            pltpu.VMEM((128, 128), F32),
            pltpu.VMEM((16, 8, 128), F32),
            pltpu.VMEM((4, 2, 4, 4, 4, 16, 128), BF16),
            pltpu.VMEM((1, D), F32),
            pltpu.VMEM((3, 64, wide), F32),
            pltpu.VMEM((3, 64, wide), BF16),
            pltpu.VMEM((3, 64, wide), BF16),
            pltpu.VMEM((3, 4, 16, wide), BF16),
            pltpu.VMEM((3, 3, 16, wide), BF16),
            pltpu.VMEM((16 * SPAN, 128), F32),
            pltpu.VMEM((3, 4, 4 * SPAN, 128), BF16),
            pltpu.VMEM((3, 3, 4 * SPAN, 128), BF16),
            pltpu.VMEM((3, 4, SPAN, 128), F32),
            pltpu.VMEM((3, 3, SPAN, 128), F32),
            pltpu.VMEM((D // 128, 128), F32),
            dma((NCHUNK + 11,)),
            dma((15,)), dma((15,)), dma((15,)), dma((15,)),
            dma((7,)), dma((7,)), dma((15,)), dma((15,)),
            dma((7,)), dma((7,)), dma((15,)), dma((15,)),
            dma((36,)), dma((36,)), dma((16,)), dma((16,)),
            dma((6,)), dma((6,)), dma((18,)), dma((18,)), dma((9,)), dma((9,)), dma((9,)), dma((9,)),
        ],
        compiler_params=pltpu.CompilerParams(
            collective_id=0, has_side_effects=True, vmem_limit_bytes=56 * 1024 * 1024
        ),
    )(
        lengths, expert_ids, route_weights, residual, query_latent, norm_gain.reshape(1, D),
        latent_cache.swapaxes(1, 2), w_uv, w_o, w_gate.reshape(D, FF), w_up.reshape(D, FF), w_down.reshape(FF, D),
    )
    return out.reshape(1, D)


def solution(mesh):
    return jax.shard_map(
        on_device,
        mesh=mesh,
        in_specs=(
            P(("dp", "tensor"), None),
            P(("dp", "tensor"), None, None),
            P(("dp", "tensor"), None, None),
            P(("dp", "tensor")),
            P("tensor", None, None),
            P("tensor", "dp", None),
            P(),
            P(("dp", "tensor"), None),
            P(("dp", "tensor"), None),
            P("dp", None, "tensor"),
            P("dp", None, "tensor"),
            P("dp", "tensor", None),
        ),
        out_specs=P(("dp", "tensor"), None),
        check_vma=False,
    )
```

```python
import jax
import jax.numpy as jnp
from jax import lax
from jax.experimental import pallas as pl
from jax.experimental.pallas import tpu as pltpu
from jax.sharding import PartitionSpec as P

MESH = pl.DeviceIdType.MESH
F32 = jnp.float32
BF16 = jnp.bfloat16

CTX, CW, LAT = 4096, 576, 512
D, H, HD, FF = 7168, 64, 128, 256
CHUNK = 1024
NCHUNK = CTX // CHUNK
WIN = 512
SCALE = 192 ** (-0.5)
EPS = 1e-06
MASKED = -1e30
PARTS = ((0, 2304), (2304, 2304), (4608, 2560))
PIECES = (
    (0, 0, 1280), (1, 0, 1280), (2, 0, 1280), (0, 1280, 1024), (1, 1280, 1024), (2, 1280, 1280),
)
ORDERS = (("z", "y", "x"), ("x", "z", "y"), ("y", "x", "z"))
GATHER_ORDERS = (("z", "y", "x"), ("x", "z", "y"), ("x", "y", "z"))
TILE_ORDER = ((0, 0, 1, 2), (2, 0, 1, 2))
SPAN = 24
PLANE = (
    (2, 2), (2, 1), (1, 2), (2, 3), (3, 2), (2, 0), (0, 2), (1, 1), (3, 3), (1, 3), (3, 1),
    (1, 0), (0, 1), (3, 0), (0, 3),
)
FIRST = 7
LINE = ((2, 1), (2, 0), (1, 1), (3, 1), (1, 0), (3, 0), (0, 1))


def window_start(dp):
    return (dp // 2) * 896 + (dp % 2) * 384


def onehot(n, source):
    row = lax.broadcasted_iota(jnp.int32, (n, n), 0)
    col = lax.broadcasted_iota(jnp.int32, (n, n), 1)
    return jnp.where(col == source(row), 1.0, 0.0).astype(BF16)


def dot(a, b):
    return jnp.dot(a, b, preferred_element_type=F32)


def layer(
    len_hbm, ids_hbm, rw_hbm, res_hbm, q_hbm, gain_hbm,
    cache_hbm, wuv_hbm, wo_hbm, wg_hbm, wu_hbm, wd_hbm,
    out_ref,
    len_ref, ids_ref, rw_ref, res_ref, q_ref, gain_ref,
    cache_v, wuv_v, wg_v, wu_v, wd_v,
    s_ref, resf_v, res_recv, wo_recv, lat_send, lat_recv, vals_send, vals_all,
    rs_send, rs_recv, st_send, st_recv, x_v, ig2_v,
    d_own, c_send, c_recv, p1, p1r, q2f, q2, q2r, mix_v,
    local_sem, a2a_s, a2a_r, rb_s, rb_r, lat_s, lat_r, val_s, val_r,
    rs_s, rs_r, st_s, st_r, ag_s, ag_r, sib_s, sib_r,
    cs_s, cs_r, p1_s, p1_r, p2_s, p2_r,
):
    dp = lax.axis_index("dp")
    t = lax.axis_index("tensor")
    pos = {"x": dp // 4, "y": dp % 4, "z": t // 2, "c": t % 2}
    core = pos["c"]

    def dp_of(step):
        return lax.rem(pos["x"] + step[0], 4) * 4 + lax.rem(pos["y"] + step[1], 4)

    def t_of(step):
        return lax.rem(pos["z"] + step[0], 4) * 2 + lax.rem(core + step[1], 2)

    def at_dp(step):
        return {"dp": dp_of(step), "tensor": t}

    def at_t(step):
        return {"dp": dp, "tensor": t_of(step)}

    def along(axis, i):
        new = dict(pos)
        new[axis] = lax.rem(pos[axis] + i, 4)
        return {"dp": new["x"] * 4 + new["y"], "tensor": new["z"] * 2 + new["c"]}

    def in_plane(a, b, step):
        new = dict(pos)
        new[a] = lax.rem(pos[a] + step[0], 4)
        new[b] = lax.rem(pos[b] + step[1], 4)
        return {"dp": new["x"] * 4 + new["y"], "tensor": new["z"] * 2 + new["c"]}

    sibling = {"dp": dp, "tensor": pos["z"] * 2 + (1 - core)}

    def remote(src, dst, ss, rs, dev):
        return pltpu.make_async_remote_copy(
            src_ref=src, dst_ref=dst, send_sem=ss, recv_sem=rs, device_id=dev, device_id_type=MESH
        )

    def sent(ref, sem):
        remote(ref, ref, sem, sem, sibling).wait_send()

    def arrived(ref, sem):
        remote(ref, ref, sem, sem, sibling).wait_recv()

    barrier = pltpu.get_barrier_semaphore()
    peers = [at_dp(step) for step in PLANE] + [at_t(step) for step in LINE]
    for d in (1, 2, 3):
        for e in (1, 2, 3):
            peers += [in_plane("x", "z", (d, e)), in_plane("y", "z", (d, e))]
    for peer in peers:
        pl.semaphore_signal(barrier, inc=1, device_id=peer, device_id_type=MESH)

    def cache_copy(i):
        return pltpu.make_async_copy(
            cache_hbm.at[0, :, pl.ds(pl.multiple_of(i * CHUNK, CHUNK), CHUNK)],
            cache_v.at[i],
            local_sem.at[i],
        )

    def local(n, src, dst):
        return pltpu.make_async_copy(src, dst, local_sem.at[NCHUNK + n])

    small = [
        local(0, q_hbm.at[0], q_ref), local(1, len_hbm, len_ref), local(2, res_hbm, res_ref),
        local(3, gain_hbm, gain_ref), local(4, ids_hbm, ids_ref), local(5, rw_hbm, rw_ref),
    ]
    small[0].start()
    small[1].start()
    cache_copy(0).start()
    small[2].start()
    for i in range(1, NCHUNK):
        cache_copy(i).start()
    for copy in small[3:]:
        copy.start()
    start = pl.multiple_of(window_start(dp), 128)
    own_wo = local(6, wo_hbm.at[:, :, pl.ds(start, WIN)], wo_recv.at[:, dp])
    own_wo.start()
    wuv_copy = local(7, wuv_hbm, wuv_v)
    wuv_copy.start()

    for copy in small[:2]:
        copy.wait()
    length = len_ref[0]
    q = q_ref[...]

    def score(i, top):
        cache_copy(i).wait()
        s = dot(q, cache_v[i]) * SCALE
        slot = lax.broadcasted_iota(jnp.int32, (H, CHUNK), 1) + i * CHUNK
        s = jnp.where(slot < length, s, MASKED)
        s_ref[i] = s
        return jnp.maximum(top, jnp.max(s, axis=1, keepdims=True))

    top = jnp.full((H, 1), MASKED, F32)
    for i in range(NCHUNK):
        top = score(i, top)

    small[2].wait()
    resf_v[...] = res_ref[...].astype(F32)
    pl.semaphore_wait(barrier, 40)

    def wo_copy(n, src_dp, slot, skip):
        first = pl.multiple_of(window_start(src_dp) + skip, 128)
        return remote(
            wo_hbm.at[:, :, pl.ds(first, WIN - skip)],
            wo_recv.at[:, slot, :, pl.ds(skip, WIN - skip)],
            a2a_s.at[skip // 128], a2a_r, at_dp(PLANE[n]),
        )

    def wo_blocks(n, skip):
        return wo_recv.at[:, pl.ds(0, n), :, pl.ds(skip, WIN - skip)]

    def by_parity(odd, f):
        pl.when(odd == 0)(lambda: f(0))
        pl.when(odd == 1)(lambda: f(128))

    def res_copy(n):
        first = pl.multiple_of(window_start(dp_of(PLANE[n])), 128)
        return remote(
            resf_v.at[:, pl.ds(first, WIN)], res_recv.at[dp], rb_s, rb_r, at_dp(PLANE[n])
        )

    def send_wo(steps):
        for n in steps:
            to = dp_of(PLANE[n])
            by_parity(
                lax.rem(to, 2), lambda skip, n=n, to=to: wo_copy(n, to, dp, skip).start()
            )

    send_wo(range(FIRST))
    res_recv[dp] = resf_v[:, pl.ds(start, WIN)]
    for n in range(15):
        res_copy(n).start()

    w_copies = [local(8 + k, src, dst) for k, (src, dst) in enumerate(
        ((wg_hbm, wg_v), (wu_hbm, wu_v), (wd_hbm, wd_v)))]
    for copy in w_copies:
        copy.start()

    total = jnp.zeros((H, 1), F32)
    acc = jnp.zeros((H, LAT), F32)
    for i in range(NCHUNK):
        slot = lax.broadcasted_iota(jnp.int32, (H, CHUNK), 1) + i * CHUNK
        w = jnp.where(slot < length, jnp.exp(s_ref[i] - top), 0.0)
        total = total + jnp.sum(w, axis=1, keepdims=True)
        acc = acc + lax.dot_general(
            w.astype(BF16), cache_v[i, :LAT], (((1,), (1,)), ((), ())), preferred_element_type=F32
        )
    latent = acc / total

    for copy in small[4:]:
        copy.wait()
    lane = lax.broadcasted_iota(jnp.int32, (1, 128), 1)
    coef = jnp.zeros((1, 128), F32)
    for k in range(8):
        coef = jnp.where(jnp.bitwise_and(lane, 15) == ids_ref[0, k], rw_ref[0, k], coef)
    high = coef.astype(BF16).astype(F32)
    coef = jnp.where(lane < 16, high, jnp.where(lane < 32, coef - high, 0.0))

    lat_send[:, :, :LAT] = latent.reshape(8, 8, LAT).astype(BF16)
    lat_send[:, :, LAT:] = jnp.broadcast_to(coef.reshape(1, 1, 128), (8, 8, 128)).astype(BF16)

    def lat_copy(n):
        return remote(
            lat_send.at[t_of(LINE[n])], lat_recv.at[t], lat_s, lat_r, at_t(LINE[n])
        )

    for n in range(7):
        lat_copy(n).start()
    lat_recv[t] = lat_send[t]
    small[3].wait()
    gain = gain_ref[...]
    ig2_v[...] = 1.0 / (gain * gain)
    wuv_copy.wait()
    arrived(lat_recv.at[pl.ds(0, 7)], lat_r)

    by_head = onehot(64, lambda r: jnp.bitwise_and(r, 7) * 8 + jnp.right_shift(r, 3))
    lat = lat_recv[...].astype(F32).reshape(64, LAT + 128).astype(BF16)
    lat = dot(by_head, lat)
    pieces = [dot(lat[8 * h : 8 * h + 8, :LAT].astype(BF16), wuv_v[h]) for h in range(8)]
    pieces.append(lat[0:8, LAT:])
    vals_send[...] = jnp.concatenate(pieces, axis=1).astype(BF16)

    v1 = pos["x"] + core * (pos["y"] - pos["x"])
    v2 = pos["x"] + pos["y"] - v1

    def val_copy(k, i):
        here = vals_all.at[v2] if k else vals_all.at[v2, v1]
        dx = (1 - core) * i if k == 0 else core * i
        return remote(here, here, val_s.at[k], val_r.at[k], at_dp((dx, i - dx)))

    vals_all[v2, v1] = vals_send[...]
    for i in (2, 1, 3):
        val_copy(0, i).start()
    send_wo(range(FIRST, 15))
    arrived(vals_all.at[0, pl.ds(0, 3)], val_r.at[0])
    for i in (2, 1, 3):
        val_copy(1, i).start()
    own_wo.wait()
    by_parity(lax.rem(dp, 2), lambda skip: arrived(wo_blocks(15, skip), a2a_r))
    arrived(vals_all.at[pl.ds(0, 3)], val_r.at[1])

    def from_row(r, row_t):
        x, y = jnp.bitwise_and(jnp.right_shift(r, 2), 3), jnp.bitwise_and(r, 3)
        inner = x + core * (y - x)
        return (x + y - inner) * 32 + inner * 8 + row_t

    to_t_order = onehot(128, lambda r: from_row(r, jnp.right_shift(r, 4)))
    vals_raw = vals_all[...].astype(F32).reshape(128, 1152).astype(BF16)
    vals = dot(to_t_order, vals_raw[:, : 8 * HD]).astype(BF16)
    part = jnp.zeros((128, WIN), F32)
    for h in range(8):
        part = part + dot(
            vals[:, h * HD : (h + 1) * HD], wo_recv[h].astype(F32).reshape(128, WIN).astype(BF16)
        )
    rs_send[...] = part.astype(BF16).reshape(8, 16, WIN)

    def rs_copy(n):
        return remote(
            rs_send.at[t_of(LINE[n])], rs_recv.at[t], rs_s, rs_r, at_t(LINE[n])
        )

    for n in range(7):
        rs_copy(n).start()
    rs_recv[t] = rs_send[t]

    to_c_order = onehot(
        128,
        lambda r: from_row(
            r, jnp.bitwise_and(jnp.right_shift(r, 4), 3) * 2 + jnp.right_shift(r, 6)
        ),
    )
    coefs = dot(to_c_order, vals_raw[:, 8 * HD :])
    col = lax.broadcasted_iota(jnp.int32, (128, 128), 1)
    mine = (col == dp) | (col == dp + 16)
    coef_col = jnp.sum(jnp.where(mine, coefs, 0.0), axis=1, keepdims=True)

    arrived(res_recv.at[pl.ds(0, 15)], rb_r)
    res = jnp.concatenate([res_recv[k] for k in range(16)], axis=0)

    arrived(rs_recv.at[pl.ds(0, 7)], rs_r)
    stream = res
    for k in range(8):
        stream = stream + rs_recv[k].astype(F32)
    scaled = (stream * gain_ref[:, pl.ds(start, WIN)]).astype(BF16)

    def either(c, f):
        zero, one = f(0), f(1)
        return zero + c * (one - zero)

    def axis_of(j, c, k):
        return GATHER_ORDERS[TILE_ORDER[c][j]][k]

    def place(j, k, c):
        return either(c, lambda v: pos[axis_of(j, v, k)])

    def block(j, phase, c, i):
        at = [place(j, k, c) for k in (2, 1, 0)][: 3 - phase]
        at[-1] = lax.rem(at[-1] - i + 4, 4)
        return x_v.at[(j, c, *at)]

    def partner(j, k, i):
        return {
            name: either(core, lambda v, name=name: along(axis_of(j, v, k), i)[name])
            for name in ("dp", "tensor")
        }

    def spread(j):
        def go():
            here = x_v.at[j, core, place(j, 2, core), place(j, 1, core), place(j, 0, core)]
            for step in PLANE:
                target = {
                    name: either(
                        core,
                        lambda v, name=name: in_plane(axis_of(j, v, 0), axis_of(j, v, 1), step)[name],
                    )
                    for name in ("dp", "tensor")
                }
                remote(
                    here, here, ag_s.at[0 if j else 1], ag_r.at[j * 7 + step[1]], target
                ).start()

        if j == 0:
            pl.when(lax.rem(pos["y"], 2) == 0)(go)
        else:
            go()

    def rows_on(j, back):
        def go():
            n = 4 if back else 3
            arrived(x_v.at[0, 0, 0, 0, pl.ds(0, n)], ag_r.at[j * 7 + back])
            row = lax.rem(place(j, 1, core) - back + 4, 4)
            here = x_v.at[j, core, place(j, 2, core), row]
            for i in (2, 1, 3):
                remote(
                    here, here, ag_s.at[3 if j == 0 else 2], ag_r.at[j * 7 + 3 + i], partner(j, 2, i)
                ).start()

        if j == 0:
            pl.when(lax.rem(pos["y"] - back + 4, 2) == 0)(go)
        else:
            go()

    def to_sibling(j, i):
        there = block(j, 2, core, i)
        return remote(there, there, sib_s, sib_r, sibling)

    for j in range(4):
        x_v[j, core, place(j, 2, core), place(j, 1, core), place(j, 0, core)] = scaled[
            :, 128 * j : 128 * j + 128
        ]
    for j in (1, 2, 3, 0):
        spread(j)

    st_send[...] = jnp.zeros_like(st_send)
    for j in range(4):
        st_send[pl.ds(j, 16, stride=8), :] = stream[:, 128 * j : 128 * j + 128]
    st_recv[dp] = st_send[pl.ds(pl.multiple_of(dp * 8, 8), 8), :]

    def st_copy(n):
        there = pl.multiple_of(dp_of(PLANE[n]) * 8, 8)
        return remote(
            st_send.at[pl.ds(there, 8)], st_recv.at[dp], st_s, st_r, at_dp(PLANE[n])
        )

    for back in (0, 1, 3, 2):
        for j in (1, 2, 3, 0):
            rows_on(j, back)
    for j in (1, 2, 3, 0):
        to_sibling(j, 0).start()

    for n in range(15):
        st_copy(n).start()

    def wo_sent(skip):
        for n, other in ((7, skip), (8, 128 - skip)):
            sent(wo_blocks(n, other), a2a_s.at[other // 128])

    by_parity(lax.rem(dp, 2), wo_sent)
    sent(res_recv.at[pl.ds(0, 15)], rb_s)
    sent(vals_all.at[0, pl.ds(0, 3)], val_s.at[0])
    sent(vals_all.at[pl.ds(0, 3)], val_s.at[1])
    sent(lat_recv.at[pl.ds(0, 7)], lat_s)
    sent(rs_recv.at[pl.ds(0, 7)], rs_s)

    for i in (1, 3, 2):
        for j in (0, 1, 2, 3):
            arrived(x_v.at[0, 0, 0] if j else x_v.at[0, 0, 0, pl.ds(0, 2)], ag_r.at[j * 7 + 3 + i])
            to_sibling(j, i).start()
    arrived(x_v.at[:, 0], sib_r)
    for copy in w_copies:
        copy.wait()

    def tile_of(j, x, y):
        halves = []
        for c in range(2):
            at = {"x": x, "y": y, "z": slice(None)}
            i1, i2, i3 = (at[a] for a in GATHER_ORDERS[TILE_ORDER[c][j]])
            halves.append(x_v[j, c, i3, i2, i1].reshape(64, 128))
        return jnp.concatenate(halves, axis=0)

    def up_step(k, carry):
        g, u, sq = carry
        tiles = []
        for odd in range(2):
            for j in range(odd, 4):
                tiles.append(tile_of(j, k // 2, 2 * lax.rem(k, 2) + odd))
        for n, tile in enumerate(tiles):
            f = tile.astype(F32)
            sq = sq + f * f * ig2_v[:, pl.ds(pl.multiple_of(k * 896 + n * 128, 128), 128)]
        x = jnp.concatenate(tiles, axis=1)
        rows = pl.ds(pl.multiple_of(k * 896, 896), 896)
        return g + dot(x, wg_v[rows, :]), u + dot(x, wu_v[rows, :]), sq

    zero = jnp.zeros((128, FF), F32)
    g, u, sq = lax.fori_loop(0, 8, up_step, (zero, zero, jnp.zeros((128, 128), F32)))
    factor = lax.rsqrt(jnp.sum(sq, axis=1, keepdims=True) * (1.0 / D) + EPS)
    g = g * factor
    act = (g / (1.0 + jnp.exp(-g))) * (u * factor * coef_col)
    act = act.astype(BF16)

    bits = {"c": 6, "z": 4, "x": 2, "y": 0}
    acts = []
    for p in range(3):

        def source(r):
            src = jnp.left_shift(jnp.bitwise_xor(jnp.right_shift(r, 6), core), bits["c"])
            for a, shift in zip(ORDERS[p], (4, 2, 0)):
                src = src + jnp.left_shift(jnp.bitwise_and(jnp.right_shift(r, shift), 3), bits[a])
            return src

        acts.append(dot(onehot(128, source), act).astype(BF16))

    def core_copy(s):
        p, at, w = PIECES[s]
        cols = pl.ds(at, w)
        return remote(
            c_send.at[p, :, cols], c_recv.at[p, :, cols], cs_s, cs_r.at[s], sibling
        )

    def sum1(s, i):
        p, at, w = PIECES[s]
        axis = ORDERS[p][0]
        cols = pl.ds(at, w)
        return remote(
            p1.at[p, lax.rem(pos[axis] + i, 4), :, cols], p1r.at[p, i - 1, :, cols],
            p1_s, p1_r.at[p], along(axis, i),
        )

    def down(s):
        p, at, w = PIECES[s]
        first = PARTS[p][0] + at
        o = dot(acts[p], wd_v[:, first : first + w])
        d_own[p, :, at : at + w] = o[:64]
        c_send[p, :, at : at + w] = o[64:].astype(BF16)
        core_copy(s).start()

    def pair(s):
        p, at, w = PIECES[s]
        core_copy(s).wait_recv()
        o = d_own[p, :, at : at + w] + c_recv[p, :, at : at + w].astype(F32)
        p1[p, :, :, at : at + w] = o.reshape(4, 16, w).astype(BF16)
        for i in (2, 1, 3):
            sum1(s, i).start()

    for s in range(len(PIECES) + 2):
        if s < len(PIECES):
            down(s)
        if s >= 2:
            pair(s - 2)

    def my_row(p):
        return pos[ORDERS[p][1]] * 4 + pos[ORDERS[p][2]]

    def row_copy(p, step):
        a, b = ORDERS[p][1], ORDERS[p][2]
        there = lax.rem(pos[a] + step[0], 4) * 4 + lax.rem(pos[b] + step[1], 4)
        return remote(
            q2.at[p, there], q2r.at[p, my_row(p)], p2_s, p2_r.at[p], in_plane(a, b, step)
        )

    q2f[...] = jnp.zeros_like(q2f)
    for p, (first, w) in enumerate(PARTS):
        arrived(p1r.at[p, :, :, pl.ds(0, w)], p1_r.at[p])
        o = p1[p, pos[ORDERS[p][0]], :, 0:w].astype(F32)
        for i in range(3):
            o = o + p1r[p, i, :, 0:w].astype(F32)
        for j in range(w // 128):
            q2f[pl.ds(j, 16, stride=SPAN), :] = o[:, 128 * j : 128 * j + 128]
        q2[p] = q2f[...].reshape(16, SPAN, 128).astype(BF16)
        for step in PLANE:
            row_copy(p, step).start()
        q2r[p, my_row(p)] = q2[p, my_row(p)]

    arrived(st_recv.at[pl.ds(0, 15)], st_r)
    sent(st_recv.at[pl.ds(0, 15)], st_s)
    for k in range(8):
        mix_v[7 * k : 7 * k + 4, :] = st_recv[2 * k, 0:4, :]
        mix_v[7 * k + 4 : 7 * k + 7, :] = st_recv[2 * k + 1, 1:4, :]

    sent(q2f.at[pl.ds(0, 360)], ag_s.at[0])

    @pl.when(lax.rem(pos["y"], 2) == 0)
    def _():
        sent(q2f.at[pl.ds(0, 120)], ag_s.at[1])

    sent(x_v.at[pl.ds(0, 3), 0, pl.ds(0, 3)], ag_s.at[2])
    sent(x_v.at[pl.ds(0, 2), 0, 0, pl.ds(0, 3)], ag_s.at[3])
    sent(x_v.at[:, 0], sib_s)
    sent(wd_v.at[pl.ds(0, 64)], cs_s)
    sent(wd_v.at[pl.ds(0, 48)], p1_s)

    for p, (first, w) in enumerate(PARTS):
        arrived(q2r.at[p, pl.ds(0, 15)], p2_r.at[p])
        o = q2r[p, 0].astype(F32)
        for i in range(1, 16):
            o = o + q2r[p, i].astype(F32)
        tiles = slice(first // 128, (first + w) // 128)
        mix_v[tiles, :] = mix_v[tiles, :] + o[: w // 128]
    out_ref[...] = mix_v[...].astype(BF16)
    sent(q2r.at[:, pl.ds(0, 15)], p2_s)


def on_device(
    residual, query_latent, latent_cache, lengths, w_uv, w_o, norm_gain, expert_ids, route_weights,
    w_gate, w_up, w_down,
):
    dma = pltpu.SemaphoreType.DMA
    vmem = pl.BlockSpec(memory_space=pltpu.VMEM)
    hbm = pl.BlockSpec(memory_space=pl.ANY)
    wide = max(w for _, w in PARTS)
    out = pl.pallas_call(
        layer,
        out_shape=jax.ShapeDtypeStruct((D // 128, 128), BF16),
        in_specs=[hbm] * 12,
        out_specs=vmem,
        scratch_shapes=[
            pltpu.SMEM((1,), jnp.int32),
            pltpu.SMEM((1, 8), jnp.int32),
            pltpu.SMEM((1, 8), F32),
            pltpu.VMEM((1, D), BF16),
            pltpu.VMEM((H, CW), BF16),
            pltpu.VMEM((1, D), F32),
            pltpu.VMEM((NCHUNK, CW, CHUNK), BF16),
            pltpu.VMEM((8, LAT, HD), BF16),
            pltpu.VMEM((D, FF), BF16),
            pltpu.VMEM((D, FF), BF16),
            pltpu.VMEM((FF, D), BF16),
            pltpu.VMEM((NCHUNK, H, CHUNK), F32),
            pltpu.VMEM((1, D), F32),
            pltpu.VMEM((16, 1, WIN), F32),
            pltpu.VMEM((8, 16, 8, WIN), BF16),
            pltpu.VMEM((8, 8, LAT + 128), BF16),
            pltpu.VMEM((8, 8, LAT + 128), BF16),
            pltpu.VMEM((8, 1152), BF16),
            pltpu.VMEM((4, 4, 8, 1152), BF16),
            pltpu.VMEM((8, 16, WIN), BF16),
            pltpu.VMEM((8, 16, WIN), BF16),
            pltpu.VMEM((128, 128), F32),
            pltpu.VMEM((16, 8, 128), F32),
            pltpu.VMEM((4, 2, 4, 4, 4, 16, 128), BF16),
            pltpu.VMEM((1, D), F32),
            pltpu.VMEM((3, 64, wide), F32),
            pltpu.VMEM((3, 64, wide), BF16),
            pltpu.VMEM((3, 64, wide), BF16),
            pltpu.VMEM((3, 4, 16, wide), BF16),
            pltpu.VMEM((3, 3, 16, wide), BF16),
            pltpu.VMEM((16 * SPAN, 128), F32),
            pltpu.VMEM((3, 16, SPAN, 128), BF16),
            pltpu.VMEM((3, 16, SPAN, 128), BF16),
            pltpu.VMEM((D // 128, 128), F32),
            dma((NCHUNK + 11,)),
            dma((2,)), dma, dma, dma, dma, dma, dma((2,)), dma((2,)),
            dma, dma, dma, dma, dma((4,)), dma((28,)), dma, dma,
            dma, dma((6,)), dma, dma((3,)), dma, dma((3,)),
        ],
        compiler_params=pltpu.CompilerParams(
            collective_id=0, has_side_effects=True, vmem_limit_bytes=56 * 1024 * 1024
        ),
    )(
        lengths, expert_ids, route_weights, residual, query_latent, norm_gain.reshape(1, D),
        latent_cache.swapaxes(1, 2), w_uv, w_o, w_gate.reshape(D, FF), w_up.reshape(D, FF), w_down.reshape(FF, D),
    )
    return out.reshape(1, D)


def solution(mesh):
    return jax.shard_map(
        on_device,
        mesh=mesh,
        in_specs=(
            P(("dp", "tensor"), None),
            P(("dp", "tensor"), None, None),
            P(("dp", "tensor"), None, None),
            P(("dp", "tensor")),
            P("tensor", None, None),
            P("tensor", "dp", None),
            P(),
            P(("dp", "tensor"), None),
            P(("dp", "tensor"), None),
            P("dp", None, "tensor"),
            P("dp", None, "tensor"),
            P("dp", "tensor", None),
        ),
        out_specs=P(("dp", "tensor"), None),
        check_vma=False,
    )
```

```python
import jax
import jax.numpy as jnp
from jax import lax
from jax.experimental import pallas as pl
from jax.experimental.pallas import tpu as pltpu
from jax.sharding import PartitionSpec as P

MESH = pl.DeviceIdType.MESH
F32 = jnp.float32
BF16 = jnp.bfloat16

CTX, CW, LAT = 4096, 576, 512
D, H, HD, FF = 7168, 64, 128, 256
CHUNK = 1024
NCHUNK = CTX // CHUNK
WIN = 512
HALF = 256
SCALE = 192 ** (-0.5)
EPS = 1e-06
MASKED = -1e30
PARTS = ((0, 2432), (2432, 2432), (4864, 2304))
DIRECT = 768
PIECES = ((0, 768, 1664), (1, 768, 1664), (2, 768, 1536))
ORDERS = (("z", "y", "x"), ("x", "z", "y"), ("y", "x", "z"))
GATHER_ORDERS = (("z", "y", "x"), ("x", "z", "y"), ("x", "y", "z"))
TILE_ORDER = ((2, 0, 0, 1), (0, 1, 2, 2))
SPAN = 24
PLANE = (
    (2, 2), (2, 1), (1, 2), (2, 3), (3, 2), (2, 0), (0, 2), (1, 1), (3, 3), (1, 3), (3, 1),
    (1, 0), (0, 1), (3, 0), (0, 3),
)
FIRST = 5
LINE = ((2, 1), (2, 0), (1, 1), (3, 1), (1, 0), (3, 0), (0, 1))


def window_start(dp):
    return (dp // 2) * 896 + (dp % 2) * 384


def onehot(n, source):
    row = lax.broadcasted_iota(jnp.int32, (n, n), 0)
    col = lax.broadcasted_iota(jnp.int32, (n, n), 1)
    return jnp.where(col == source(row), 1.0, 0.0).astype(BF16)


def dot(a, b):
    return jnp.dot(a, b, preferred_element_type=F32)


def layer(
    len_hbm, ids_hbm, rw_hbm, res_hbm, q_hbm, gain_hbm,
    cache_hbm, wuv_hbm, wo_hbm, wg_hbm, wu_hbm, wd_hbm,
    out_ref,
    len_ref, ids_ref, rw_ref, res_ref, q_ref, gain_ref,
    cache_v, wuv_v, wg_v, wu_v, wd_v,
    s_ref, resf_v, res_recv, wo_recv, lat_send, lat_recv, vals_send, vals_all,
    rs_send, rs_recv, st_send, st_recv, x_v, ig2_v,
    d_own, c_send, c_recv, p1, p1r, q2f, q2, q2r, mix_v, order_v, pd, pdr,
    local_sem, a2a_s, a2a_r, rb_s, rb_r, lat_s, lat_r, val_s, val_r,
    rs_s, rs_r, st_s, st_r, ag_s, ag_r, sib_s, sib_r,
    cs_s, cs_r, p1_s, p1_r, p2_s, p2_r, pd_s, pd_r,
):
    dp = lax.axis_index("dp")
    t = lax.axis_index("tensor")
    pos = {"x": dp // 4, "y": dp % 4, "z": t // 2, "c": t % 2}
    core = pos["c"]

    def dp_of(step):
        return lax.rem(pos["x"] + step[0], 4) * 4 + lax.rem(pos["y"] + step[1], 4)

    def t_of(step):
        return lax.rem(pos["z"] + step[0], 4) * 2 + lax.rem(core + step[1], 2)

    def at_dp(step):
        return {"dp": dp_of(step), "tensor": t}

    def at_t(step):
        return {"dp": dp, "tensor": t_of(step)}

    def along(axis, i):
        new = dict(pos)
        new[axis] = lax.rem(pos[axis] + i, 4)
        return {"dp": new["x"] * 4 + new["y"], "tensor": new["z"] * 2 + new["c"]}

    def in_plane(a, b, step):
        new = dict(pos)
        new[a] = lax.rem(pos[a] + step[0], 4)
        new[b] = lax.rem(pos[b] + step[1], 4)
        return {"dp": new["x"] * 4 + new["y"], "tensor": new["z"] * 2 + new["c"]}

    def crossed(device):
        return {"dp": device["dp"], "tensor": device["tensor"] + 1 - 2 * core}

    sibling = {"dp": dp, "tensor": pos["z"] * 2 + (1 - core)}

    def remote(src, dst, ss, rs, dev):
        return pltpu.make_async_remote_copy(
            src_ref=src, dst_ref=dst, send_sem=ss, recv_sem=rs, device_id=dev, device_id_type=MESH
        )

    def sent(ref, sem):
        remote(ref, ref, sem, sem, sibling).wait_send()

    def arrived(ref, sem):
        remote(ref, ref, sem, sem, sibling).wait_recv()

    barrier = pltpu.get_barrier_semaphore()
    peers = [at_dp(step) for step in PLANE] + [at_t(step) for step in LINE]
    for d in (1, 2, 3):
        for e in (1, 2, 3):
            peers += [in_plane("x", "z", (d, e)), in_plane("y", "z", (d, e))]
        peers += [crossed(along("x", d)), crossed(along("y", d))]
    for peer in peers:
        pl.semaphore_signal(barrier, inc=1, device_id=peer, device_id_type=MESH)

    def cache_copy(i):
        return pltpu.make_async_copy(
            cache_hbm.at[0, :, pl.ds(pl.multiple_of(i * CHUNK, CHUNK), CHUNK)],
            cache_v.at[i],
            local_sem.at[i],
        )

    def local(n, src, dst):
        return pltpu.make_async_copy(src, dst, local_sem.at[NCHUNK + n])

    small = [
        local(0, q_hbm.at[0], q_ref), local(1, len_hbm, len_ref), local(2, res_hbm, res_ref),
        local(3, gain_hbm, gain_ref), local(4, ids_hbm, ids_ref), local(5, rw_hbm, rw_ref),
    ]
    small[0].start()
    small[1].start()
    cache_copy(0).start()
    small[2].start()
    for i in range(1, NCHUNK):
        cache_copy(i).start()
    for copy in small[3:]:
        copy.start()
    start = pl.multiple_of(window_start(dp), 128)
    own_wo = local(6, wo_hbm.at[:, :, pl.ds(start, WIN)], wo_recv.at[:, dp])
    own_wo.start()
    wuv_copy = local(7, wuv_hbm, wuv_v)
    wuv_copy.start()

    for copy in small[:2]:
        copy.wait()
    length = len_ref[0]
    q = q_ref[...]

    def score(i, top):
        cache_copy(i).wait()
        s = dot(q, cache_v[i]) * SCALE
        slot = lax.broadcasted_iota(jnp.int32, (H, CHUNK), 1) + i * CHUNK
        s = jnp.where(slot < length, s, MASKED)
        s_ref[i] = s
        return jnp.maximum(top, jnp.max(s, axis=1, keepdims=True))

    top = jnp.full((H, 1), MASKED, F32)
    for i in range(NCHUNK):
        top = score(i, top)

    small[2].wait()
    resf_v[...] = res_ref[...].astype(F32)
    pl.semaphore_wait(barrier, 46)

    def wo_copy(n, src_dp, slot, lo, hi, ss, rs):
        first = pl.multiple_of(window_start(src_dp) + lo, 128)
        return remote(
            wo_hbm.at[:, :, pl.ds(first, hi - lo)], wo_recv.at[:, slot, :, pl.ds(lo, hi - lo)],
            ss, rs, at_dp(PLANE[n]),
        )

    def wo_blocks(n, lo, hi):
        return wo_recv.at[:, pl.ds(0, n), :, pl.ds(lo, hi - lo)]

    def by_parity(odd, f):
        pl.when(odd == 0)(lambda: f(0))
        pl.when(odd == 1)(lambda: f(128))

    def res_copy(n):
        first = pl.multiple_of(window_start(dp_of(PLANE[n])), 128)
        return remote(
            resf_v.at[:, pl.ds(first, WIN)], res_recv.at[dp], rb_s, rb_r, at_dp(PLANE[n])
        )

    def send_low(steps):
        for n in steps:
            to = dp_of(PLANE[n])
            by_parity(
                lax.rem(to, 2),
                lambda skip, n=n, to=to: wo_copy(
                    n, to, dp, skip, HALF, a2a_s.at[skip // 128], a2a_r.at[0]
                ).start(),
            )

    for n in range(15):
        wo_copy(n, dp_of(PLANE[n]), dp, HALF, WIN, a2a_s.at[2], a2a_r.at[1]).start()
    res_recv[dp] = resf_v[:, pl.ds(start, WIN)]
    w_copies = [local(8 + k, src, dst) for k, (src, dst) in enumerate(
        ((wg_hbm, wg_v), (wu_hbm, wu_v), (wd_hbm, wd_v)))]
    for copy in w_copies:
        copy.start()

    total = jnp.zeros((H, 1), F32)
    acc = jnp.zeros((H, LAT), F32)
    for i in range(NCHUNK):
        slot = lax.broadcasted_iota(jnp.int32, (H, CHUNK), 1) + i * CHUNK
        w = jnp.where(slot < length, jnp.exp(s_ref[i] - top), 0.0)
        total = total + jnp.sum(w, axis=1, keepdims=True)
        acc = acc + lax.dot_general(
            w.astype(BF16), cache_v[i, :LAT], (((1,), (1,)), ((), ())), preferred_element_type=F32
        )
    latent = acc / total

    for copy in small[4:]:
        copy.wait()
    lane = lax.broadcasted_iota(jnp.int32, (1, 128), 1)
    coef = jnp.zeros((1, 128), F32)
    for k in range(8):
        coef = jnp.where(jnp.bitwise_and(lane, 15) == ids_ref[0, k], rw_ref[0, k], coef)
    high = coef.astype(BF16).astype(F32)
    coef = jnp.where(lane < 16, high, jnp.where(lane < 32, coef - high, 0.0))

    lat_send[:, :, :LAT] = latent.reshape(8, 8, LAT).astype(BF16)
    lat_send[:, :, LAT:] = jnp.broadcast_to(coef.reshape(1, 1, 128), (8, 8, 128)).astype(BF16)

    def lat_copy(n):
        return remote(
            lat_send.at[t_of(LINE[n])], lat_recv.at[t], lat_s, lat_r, at_t(LINE[n])
        )

    for n in range(7):
        lat_copy(n).start()
    lat_recv[t] = lat_send[t]
    order_v[0, :64, :64] = onehot(
        64, lambda r: jnp.bitwise_and(r, 7) * 8 + jnp.right_shift(r, 3)
    )
    small[3].wait()
    gain = gain_ref[...]
    ig2_v[...] = 1.0 / (gain * gain)
    wuv_copy.wait()
    arrived(lat_recv.at[pl.ds(0, 7)], lat_r)

    lat = lat_recv[...].astype(F32).reshape(64, LAT + 128).astype(BF16)
    lat = dot(order_v[0, :64, :64], lat)
    pieces = [dot(lat[8 * h : 8 * h + 8, :LAT].astype(BF16), wuv_v[h]) for h in range(8)]
    pieces.append(lat[0:8, LAT:])
    vals_send[...] = jnp.concatenate(pieces, axis=1).astype(BF16)

    v1 = pos["x"] + core * (pos["y"] - pos["x"])
    v2 = pos["x"] + pos["y"] - v1

    def val_copy(k, i):
        here = vals_all.at[v2] if k else vals_all.at[v2, v1]
        dx = (1 - core) * i if k == 0 else core * i
        return remote(here, here, val_s.at[k], val_r.at[k], at_dp((dx, i - dx)))

    vals_all[v2, v1] = vals_send[...]
    for i in (2, 1, 3):
        val_copy(0, i).start()
    send_low(range(FIRST))
    def from_row(r, row_t):
        x, y = jnp.bitwise_and(jnp.right_shift(r, 2), 3), jnp.bitwise_and(r, 3)
        inner = x + core * (y - x)
        return (x + y - inner) * 32 + inner * 8 + row_t

    order_v[1] = onehot(128, lambda r: from_row(r, jnp.right_shift(r, 4)))
    order_v[2] = onehot(
        128,
        lambda r: from_row(
            r, jnp.bitwise_and(jnp.right_shift(r, 4), 3) * 2 + jnp.right_shift(r, 6)
        ),
    )
    bits = {"c": 6, "z": 4, "x": 2, "y": 0}
    for p in range(3):

        def source(r):
            src = jnp.left_shift(jnp.bitwise_xor(jnp.right_shift(r, 6), core), bits["c"])
            for a, shift in zip(ORDERS[p], (4, 2, 0)):
                src = src + jnp.left_shift(jnp.bitwise_and(jnp.right_shift(r, shift), 3), bits[a])
            return src

        order_v[3 + p] = onehot(128, source)
    arrived(vals_all.at[0, pl.ds(0, 3)], val_r.at[0])
    for i in (2, 1, 3):
        val_copy(1, i).start()
    send_low(range(FIRST, 15))
    for n in range(15):
        res_copy(n).start()
    own_wo.wait()
    arrived(wo_blocks(15, HALF, WIN), a2a_r.at[1])
    arrived(vals_all.at[pl.ds(0, 3)], val_r.at[1])

    vals_raw = vals_all[...].astype(F32).reshape(128, 1152).astype(BF16)
    vals = dot(order_v[1], vals_raw[:, : 8 * HD]).astype(BF16)

    def rs_copy(half, n):
        return remote(
            rs_send.at[half, t_of(LINE[n])], rs_recv.at[half, t],
            rs_s.at[half], rs_r.at[half], at_t(LINE[n]),
        )

    def project(half):
        part = jnp.zeros((128, HALF), F32)
        for h in range(8):
            w = wo_recv[h, :, :, half * HALF : half * HALF + HALF]
            part = part + dot(
                vals[:, h * HD : (h + 1) * HD], w.astype(F32).reshape(128, HALF).astype(BF16)
            )
        rs_send[half] = part.astype(BF16).reshape(8, 16, HALF)
        for n in range(7):
            rs_copy(half, n).start()
        rs_recv[half, t] = rs_send[half, t]

    project(1)

    coefs = dot(order_v[2], vals_raw[:, 8 * HD :])
    col = lax.broadcasted_iota(jnp.int32, (128, 128), 1)
    mine = (col == dp) | (col == dp + 16)
    coef_col = jnp.sum(jnp.where(mine, coefs, 0.0), axis=1, keepdims=True)

    by_parity(lax.rem(dp, 2), lambda skip: arrived(wo_blocks(15, skip, HALF), a2a_r.at[0]))
    project(0)

    def either(c, f):
        zero, one = f(0), f(1)
        return zero + c * (one - zero)

    def axis_of(j, c, k):
        return GATHER_ORDERS[TILE_ORDER[c][j]][k]

    def place(j, k, c):
        return either(c, lambda v: pos[axis_of(j, v, k)])

    def block(j, phase, c, i):
        at = [place(j, k, c) for k in (2, 1, 0)][: 3 - phase]
        at[-1] = lax.rem(at[-1] - i + 4, 4)
        return x_v.at[(j, c, *at)]

    def partner(j, k, i):
        return {
            name: either(core, lambda v, name=name: along(axis_of(j, v, k), i)[name])
            for name in ("dp", "tensor")
        }

    def spread(j):
        def go():
            here = x_v.at[j, core, place(j, 2, core), place(j, 1, core), place(j, 0, core)]
            for step in PLANE:
                target = {
                    name: either(
                        core,
                        lambda v, name=name: in_plane(axis_of(j, v, 0), axis_of(j, v, 1), step)[name],
                    )
                    for name in ("dp", "tensor")
                }
                remote(
                    here, here, ag_s.at[0 if j else 1], ag_r.at[j * 7 + step[1]], target
                ).start()

        if j == 0:
            pl.when(lax.rem(pos["y"], 2) == 0)(go)
        else:
            go()

    def rows_on(j, back):
        def go():
            n = 4 if back else 3
            arrived(x_v.at[0, 0, 0, 0, pl.ds(0, n)], ag_r.at[j * 7 + back])
            row = lax.rem(place(j, 1, core) - back + 4, 4)
            here = x_v.at[j, core, place(j, 2, core), row]
            for i in (2, 1, 3):
                remote(
                    here, here, ag_s.at[3 if j == 0 else 2], ag_r.at[j * 7 + 3 + i], partner(j, 2, i)
                ).start()

        if j == 0:
            pl.when(lax.rem(pos["y"] - back + 4, 2) == 0)(go)
        else:
            go()

    def to_sibling(j, i):
        there = block(j, 2, core, i)
        return remote(there, there, sib_s, sib_r, sibling)

    arrived(res_recv.at[pl.ds(0, 15)], rb_r)
    res = jnp.concatenate([res_recv[k] for k in range(16)], axis=0)
    st_send[...] = jnp.zeros_like(st_send)

    def send_half(half):
        arrived(rs_recv.at[half, pl.ds(0, 7)], rs_r.at[half])
        stream = res[:, half * HALF : half * HALF + HALF]
        for k in range(8):
            stream = stream + rs_recv[half, k].astype(F32)
        scaled = (stream * gain_ref[:, pl.ds(start + half * HALF, HALF)]).astype(BF16)
        for j in (1, 0):
            at = place(2 * half + j, 2, core), place(2 * half + j, 1, core), place(2 * half + j, 0, core)
            x_v[(2 * half + j, core, *at)] = scaled[:, 128 * j : 128 * j + 128]
            spread(2 * half + j)
        for j in range(2):
            st_send[pl.ds(2 * half + j, 16, stride=8), :] = stream[:, 128 * j : 128 * j + 128]

    send_half(1)
    send_half(0)

    st_recv[dp] = st_send[pl.ds(pl.multiple_of(dp * 8, 8), 8), :]

    def st_copy(n):
        there = pl.multiple_of(dp_of(PLANE[n]) * 8, 8)
        return remote(
            st_send.at[pl.ds(there, 8)], st_recv.at[dp], st_s, st_r, at_dp(PLANE[n])
        )

    for tiles in ((3, 2), (1, 0)):
        for back in (0, 1, 3, 2):
            for j in tiles:
                rows_on(j, back)
        for j in tiles:
            to_sibling(j, 0).start()

    for n in range(15):
        st_copy(n).start()

    def wo_sent(skip):
        for n, other in ((7, skip), (8, 128 - skip)):
            sent(wo_blocks(n, other, HALF), a2a_s.at[other // 128])

    by_parity(lax.rem(dp, 2), wo_sent)
    sent(wo_blocks(15, HALF, WIN), a2a_s.at[2])
    sent(res_recv.at[pl.ds(0, 15)], rb_s)
    sent(vals_all.at[0, pl.ds(0, 3)], val_s.at[0])
    sent(vals_all.at[pl.ds(0, 3)], val_s.at[1])
    sent(lat_recv.at[pl.ds(0, 7)], lat_s)
    for half in range(2):
        sent(rs_recv.at[half, pl.ds(0, 7)], rs_s.at[half])

    for i in (1, 3, 2):
        for j in (2, 3, 1, 0):
            arrived(x_v.at[0, 0, 0] if j else x_v.at[0, 0, 0, pl.ds(0, 2)], ag_r.at[j * 7 + 3 + i])
            to_sibling(j, i).start()
    arrived(x_v.at[:, 0], sib_r)
    for copy in w_copies:
        copy.wait()

    def tile_of(j, x, y):
        halves = []
        for c in range(2):
            at = {"x": x, "y": y, "z": slice(None)}
            i1, i2, i3 = (at[a] for a in GATHER_ORDERS[TILE_ORDER[c][j]])
            halves.append(x_v[j, c, i3, i2, i1].reshape(64, 128))
        return jnp.concatenate(halves, axis=0)

    def up_step(k, carry):
        g, u, sq = carry
        tiles = [tile_of(j, k, y) for y in range(4) for j in range(y % 2, 4)]
        for n, tile in enumerate(tiles):
            f = tile.astype(F32)
            sq = sq + f * f * ig2_v[:, pl.ds(pl.multiple_of(k * 1792 + n * 128, 128), 128)]
        x = jnp.concatenate(tiles, axis=1)
        rows = pl.ds(pl.multiple_of(k * 1792, 1792), 1792)
        return g + dot(x, wg_v[rows, :]), u + dot(x, wu_v[rows, :]), sq

    zero = jnp.zeros((128, FF), F32)
    g, u, sq = lax.fori_loop(
        0, 4, up_step, (zero, zero, jnp.zeros((128, 128), F32)), unroll=True
    )
    factor = lax.rsqrt(jnp.sum(sq, axis=1, keepdims=True) * (1.0 / D) + EPS)
    g = g * factor
    act = (g / (1.0 + jnp.exp(-g))) * (u * factor * coef_col)
    act = act.astype(BF16)

    acts = [dot(order_v[3 + p], act).astype(BF16) for p in range(3)]

    def core_copy(s):
        p, at, w = PIECES[s]
        cols = pl.ds(at, w)
        return remote(
            c_send.at[p, :, cols], c_recv.at[p, :, cols], cs_s, cs_r.at[s], sibling
        )

    def sum1(s, i):
        p, at, w = PIECES[s]
        axis = ORDERS[p][0]
        cols = pl.ds(at, w)
        return remote(
            p1.at[p, lax.rem(pos[axis] + i, 4), :, cols], p1r.at[p, i - 1, :, cols],
            p1_s, p1_r.at[p], along(axis, i),
        )

    def down(s):
        p, at, w = PIECES[s]
        first = PARTS[p][0] + at
        o = dot(acts[p], wd_v[:, first : first + w])
        d_own[p, :, at : at + w] = o[:64]
        c_send[p, :, at : at + w] = o[64:].astype(BF16)
        core_copy(s).start()

    def pair(s):
        p, at, w = PIECES[s]
        core_copy(s).wait_recv()
        o = d_own[p, :, at : at + w] + c_recv[p, :, at : at + w].astype(F32)
        p1[p, :, :, at : at + w] = o.reshape(4, 16, w).astype(BF16)
        for i in (2, 1, 3):
            sum1(s, i).start()

    def direct_copy(p, other, i):
        axis = ORDERS[p][0]
        target = along(axis, i)
        return remote(
            pd.at[p, other, lax.rem(pos[axis] + i, 4)], pdr.at[p, core * 4 + pos[axis]],
            pd_s, pd_r.at[p], crossed(target) if other else target,
        )

    def direct(p):
        first = PARTS[p][0]
        o = dot(acts[p], wd_v[:, first : first + DIRECT])
        pd[p] = o.reshape(2, 4, 16, DIRECT).astype(BF16)
        for other, i in ((1, 2), (0, 2), (1, 1), (1, 3), (0, 1), (0, 3), (1, 0)):
            direct_copy(p, other, i).start()
        pdr[p, core * 4 + pos[ORDERS[p][0]]] = pd[p, 0, pos[ORDERS[p][0]]]

    for p in range(3):
        direct(p)
    for s in range(3):
        down(s)
    for s in range(3):
        pair(s)

    def my_row(p):
        return pos[ORDERS[p][1]] * 4 + pos[ORDERS[p][2]]

    def row_copy(p, step):
        a, b = ORDERS[p][1], ORDERS[p][2]
        there = lax.rem(pos[a] + step[0], 4) * 4 + lax.rem(pos[b] + step[1], 4)
        return remote(
            q2.at[p, there], q2r.at[p, my_row(p)], p2_s, p2_r.at[p], in_plane(a, b, step)
        )

    q2f[...] = jnp.zeros_like(q2f)
    for p, (first, w) in enumerate(PARTS):
        arrived(pdr.at[p, pl.ds(0, 7)], pd_r.at[p])
        o = pdr[p, 0].astype(F32)
        for i in range(1, 8):
            o = o + pdr[p, i].astype(F32)
        arrived(p1r.at[p, :, :, pl.ds(DIRECT, w - DIRECT)], p1_r.at[p])
        rest = p1[p, pos[ORDERS[p][0]], :, DIRECT:w].astype(F32)
        for i in range(3):
            rest = rest + p1r[p, i, :, DIRECT:w].astype(F32)
        o = jnp.concatenate([o, rest], axis=1)
        for j in range(w // 128):
            q2f[pl.ds(j, 16, stride=SPAN), :] = o[:, 128 * j : 128 * j + 128]
        q2[p] = q2f[...].reshape(16, SPAN, 128).astype(BF16)
        for step in PLANE:
            row_copy(p, step).start()
        q2r[p, my_row(p)] = q2[p, my_row(p)]

    arrived(st_recv.at[pl.ds(0, 15)], st_r)
    sent(st_recv.at[pl.ds(0, 15)], st_s)
    for k in range(8):
        mix_v[7 * k : 7 * k + 4, :] = st_recv[2 * k, 0:4, :]
        mix_v[7 * k + 4 : 7 * k + 7, :] = st_recv[2 * k + 1, 1:4, :]

    sent(q2f.at[pl.ds(0, 360)], ag_s.at[0])

    @pl.when(lax.rem(pos["y"], 2) == 0)
    def _():
        sent(q2f.at[pl.ds(0, 120)], ag_s.at[1])

    sent(x_v.at[pl.ds(0, 3), 0, pl.ds(0, 3)], ag_s.at[2])
    sent(x_v.at[pl.ds(0, 2), 0, 0, pl.ds(0, 3)], ag_s.at[3])
    sent(x_v.at[:, 0], sib_s)
    sent(wd_v.at[pl.ds(0, 64), pl.ds(0, D - 3 * DIRECT)], cs_s)
    sent(wd_v.at[pl.ds(0, 48), pl.ds(0, D - 3 * DIRECT)], p1_s)
    sent(pdr.at[:, pl.ds(0, 7)], pd_s)

    for p, (first, w) in enumerate(PARTS):
        arrived(q2r.at[p, pl.ds(0, 15)], p2_r.at[p])
        o = q2r[p, 0].astype(F32)
        for i in range(1, 16):
            o = o + q2r[p, i].astype(F32)
        tiles = slice(first // 128, (first + w) // 128)
        mix_v[tiles, :] = mix_v[tiles, :] + o[: w // 128]
    out_ref[...] = mix_v[...].astype(BF16)
    sent(q2r.at[:, pl.ds(0, 15)], p2_s)


def on_device(
    residual, query_latent, latent_cache, lengths, w_uv, w_o, norm_gain, expert_ids, route_weights,
    w_gate, w_up, w_down,
):
    dma = pltpu.SemaphoreType.DMA
    vmem = pl.BlockSpec(memory_space=pltpu.VMEM)
    hbm = pl.BlockSpec(memory_space=pl.ANY)
    wide = max(w for _, w in PARTS)
    out = pl.pallas_call(
        layer,
        out_shape=jax.ShapeDtypeStruct((D // 128, 128), BF16),
        in_specs=[hbm] * 12,
        out_specs=vmem,
        scratch_shapes=[
            pltpu.SMEM((1,), jnp.int32),
            pltpu.SMEM((1, 8), jnp.int32),
            pltpu.SMEM((1, 8), F32),
            pltpu.VMEM((1, D), BF16),
            pltpu.VMEM((H, CW), BF16),
            pltpu.VMEM((1, D), F32),
            pltpu.VMEM((NCHUNK, CW, CHUNK), BF16),
            pltpu.VMEM((8, LAT, HD), BF16),
            pltpu.VMEM((D, FF), BF16),
            pltpu.VMEM((D, FF), BF16),
            pltpu.VMEM((FF, D), BF16),
            pltpu.VMEM((NCHUNK, H, CHUNK), F32),
            pltpu.VMEM((1, D), F32),
            pltpu.VMEM((16, 1, WIN), F32),
            pltpu.VMEM((8, 16, 8, WIN), BF16),
            pltpu.VMEM((8, 8, LAT + 128), BF16),
            pltpu.VMEM((8, 8, LAT + 128), BF16),
            pltpu.VMEM((8, 1152), BF16),
            pltpu.VMEM((4, 4, 8, 1152), BF16),
            pltpu.VMEM((2, 8, 16, HALF), BF16),
            pltpu.VMEM((2, 8, 16, HALF), BF16),
            pltpu.VMEM((128, 128), F32),
            pltpu.VMEM((16, 8, 128), F32),
            pltpu.VMEM((4, 2, 4, 4, 4, 16, 128), BF16),
            pltpu.VMEM((1, D), F32),
            pltpu.VMEM((3, 64, wide), F32),
            pltpu.VMEM((3, 64, wide), BF16),
            pltpu.VMEM((3, 64, wide), BF16),
            pltpu.VMEM((3, 4, 16, wide), BF16),
            pltpu.VMEM((3, 3, 16, wide), BF16),
            pltpu.VMEM((16 * SPAN, 128), F32),
            pltpu.VMEM((3, 16, SPAN, 128), BF16),
            pltpu.VMEM((3, 16, SPAN, 128), BF16),
            pltpu.VMEM((D // 128, 128), F32),
            pltpu.VMEM((6, 128, 128), BF16),
            pltpu.VMEM((3, 2, 4, 16, DIRECT), BF16),
            pltpu.VMEM((3, 8, 16, DIRECT), BF16),
            dma((NCHUNK + 11,)),
            dma((3,)), dma((2,)), dma, dma, dma, dma, dma((2,)), dma((2,)),
            dma((2,)), dma((2,)), dma, dma, dma((4,)), dma((28,)), dma, dma,
            dma, dma((3,)), dma, dma((3,)), dma, dma((3,)), dma, dma((3,)),
        ],
        compiler_params=pltpu.CompilerParams(
            collective_id=0, has_side_effects=True, vmem_limit_bytes=56 * 1024 * 1024
        ),
    )(
        lengths, expert_ids, route_weights, residual, query_latent, norm_gain.reshape(1, D),
        latent_cache.swapaxes(1, 2), w_uv, w_o, w_gate.reshape(D, FF), w_up.reshape(D, FF), w_down.reshape(FF, D),
    )
    return out.reshape(1, D)


def solution(mesh):
    return jax.shard_map(
        on_device,
        mesh=mesh,
        in_specs=(
            P(("dp", "tensor"), None),
            P(("dp", "tensor"), None, None),
            P(("dp", "tensor"), None, None),
            P(("dp", "tensor")),
            P("tensor", None, None),
            P("tensor", "dp", None),
            P(),
            P(("dp", "tensor"), None),
            P(("dp", "tensor"), None),
            P("dp", None, "tensor"),
            P("dp", None, "tensor"),
            P("dp", "tensor", None),
        ),
        out_specs=P(("dp", "tensor"), None),
        check_vma=False,
    )
```

```python
import jax
import jax.numpy as jnp
from jax import lax
from jax.experimental import pallas as pl
from jax.experimental.pallas import tpu as pltpu
from jax.sharding import PartitionSpec as P

MESH = pl.DeviceIdType.MESH
F32 = jnp.float32
BF16 = jnp.bfloat16

CTX, CW, LAT = 4096, 576, 512
D, H, HD, FF = 7168, 64, 128, 256
CHUNK = 1024
NCHUNK = CTX // CHUNK
WIN = 512
HALF = 256
SCALE = 192 ** (-0.5)
EPS = 1e-06
MASKED = -1e30
PARTS = ((0, 2432), (2432, 2432), (4864, 2304))
DIRECT = 768
PIECES = ((0, 768, 1664), (1, 768, 1664), (2, 768, 1536))
ORDERS = (("z", "y", "x"), ("x", "z", "y"), ("y", "x", "z"))
GATHER_ORDERS = (("z", "y", "x"), ("x", "z", "y"), ("x", "y", "z"))
TILE_ORDER = ((2, 0, 0, 1), (0, 1, 2, 2))
SPAN = 24
PLANE = (
    (2, 2), (2, 1), (1, 2), (2, 3), (3, 2), (2, 0), (0, 2), (1, 1), (3, 3), (1, 3), (3, 1),
    (1, 0), (0, 1), (3, 0), (0, 3),
)
FIRST = 5
LINE = ((2, 1), (2, 0), (1, 1), (3, 1), (1, 0), (3, 0), (0, 1))


def window_start(dp):
    return (dp // 2) * 896 + (dp % 2) * 384


def onehot(n, source):
    row = lax.broadcasted_iota(jnp.int32, (n, n), 0)
    col = lax.broadcasted_iota(jnp.int32, (n, n), 1)
    return jnp.where(col == source(row), 1.0, 0.0).astype(BF16)


def dot(a, b):
    return jnp.dot(a, b, preferred_element_type=F32)


def layer(
    len_hbm, ids_hbm, rw_hbm, res_hbm, q_hbm, gain_hbm,
    cache_hbm, wuv_hbm, wo_hbm, wg_hbm, wu_hbm, wd_hbm,
    out_ref,
    len_ref, ids_ref, rw_ref, res_ref, q_ref, gain_ref,
    cache_v, wuv_v, wg_v, wu_v, wd_v,
    s_ref, resf_v, res_recv, wo_recv, lat_send, lat_recv, vals_send, vals_all,
    rs_send, rs_recv, st_send, st_recv, x_v, ig2_v,
    d_own, c_send, c_recv, p1, p1r, q2f, q2, q2r, mix_v, order_v, pd, pdr,
    local_sem, a2a_s, a2a_r, rb_s, rb_r, lat_s, lat_r, val_s, val_r,
    rs_s, rs_r, st_s, st_r, ag_s, ag_r, sib_s, sib_r,
    cs_s, cs_r, p1_s, p1_r, p2_s, p2_r, pd_s, pd_r,
):
    dp = lax.axis_index("dp")
    t = lax.axis_index("tensor")
    pos = {"x": dp // 4, "y": dp % 4, "z": t // 2, "c": t % 2}
    core = pos["c"]

    def dp_of(step):
        return lax.rem(pos["x"] + step[0], 4) * 4 + lax.rem(pos["y"] + step[1], 4)

    def t_of(step):
        return lax.rem(pos["z"] + step[0], 4) * 2 + lax.rem(core + step[1], 2)

    def at_dp(step):
        return {"dp": dp_of(step), "tensor": t}

    def at_t(step):
        return {"dp": dp, "tensor": t_of(step)}

    def along(axis, i):
        new = dict(pos)
        new[axis] = lax.rem(pos[axis] + i, 4)
        return {"dp": new["x"] * 4 + new["y"], "tensor": new["z"] * 2 + new["c"]}

    def in_plane(a, b, step):
        new = dict(pos)
        new[a] = lax.rem(pos[a] + step[0], 4)
        new[b] = lax.rem(pos[b] + step[1], 4)
        return {"dp": new["x"] * 4 + new["y"], "tensor": new["z"] * 2 + new["c"]}

    def crossed(device):
        return {"dp": device["dp"], "tensor": device["tensor"] + 1 - 2 * core}

    sibling = {"dp": dp, "tensor": pos["z"] * 2 + (1 - core)}

    def remote(src, dst, ss, rs, dev):
        return pltpu.make_async_remote_copy(
            src_ref=src, dst_ref=dst, send_sem=ss, recv_sem=rs, device_id=dev, device_id_type=MESH
        )

    def sent(ref, sem):
        remote(ref, ref, sem, sem, sibling).wait_send()

    def arrived(ref, sem):
        remote(ref, ref, sem, sem, sibling).wait_recv()

    def cache_copy(i):
        return pltpu.make_async_copy(
            cache_hbm.at[0, :, pl.ds(pl.multiple_of(i * CHUNK, CHUNK), CHUNK)],
            cache_v.at[i],
            local_sem.at[i],
        )

    def local(n, src, dst):
        return pltpu.make_async_copy(src, dst, local_sem.at[NCHUNK + n])

    small = [
        local(0, q_hbm.at[0], q_ref), local(1, len_hbm, len_ref), local(2, res_hbm, res_ref),
        local(3, gain_hbm, gain_ref), local(4, ids_hbm, ids_ref), local(5, rw_hbm, rw_ref),
    ]
    small[0].start()
    small[1].start()
    cache_copy(0).start()
    small[2].start()
    for i in range(1, NCHUNK):
        cache_copy(i).start()
    for copy in small[3:]:
        copy.start()
    barrier = pltpu.get_barrier_semaphore()
    peers = [at_dp(step) for step in PLANE] + [at_t(step) for step in LINE]
    for d in (1, 2, 3):
        for e in (1, 2, 3):
            peers += [in_plane("x", "z", (d, e)), in_plane("y", "z", (d, e))]
        peers += [crossed(along("x", d)), crossed(along("y", d))]
    for peer in peers:
        pl.semaphore_signal(barrier, inc=1, device_id=peer, device_id_type=MESH)

    start = pl.multiple_of(window_start(dp), 128)
    own_wo = local(6, wo_hbm.at[:, :, pl.ds(start, WIN)], wo_recv.at[:, dp])
    own_wo.start()
    wuv_copy = local(7, wuv_hbm, wuv_v)
    wuv_copy.start()

    for copy in small[:2]:
        copy.wait()
    length = len_ref[0]
    q = q_ref[...]

    def score(i, top):
        cache_copy(i).wait()
        s = dot(q, cache_v[i]) * SCALE
        slot = lax.broadcasted_iota(jnp.int32, (H, CHUNK), 1) + i * CHUNK
        s = jnp.where(slot < length, s, MASKED)
        s_ref[i] = s
        return jnp.maximum(top, jnp.max(s, axis=1, keepdims=True))

    top = jnp.full((H, 1), MASKED, F32)
    for i in range(NCHUNK):
        top = score(i, top)

    small[2].wait()
    resf_v[...] = res_ref[...].astype(F32)
    pl.semaphore_wait(barrier, 46)

    def wo_copy(n, src_dp, slot, lo, hi, ss, rs):
        first = pl.multiple_of(window_start(src_dp) + lo, 128)
        return remote(
            wo_hbm.at[:, :, pl.ds(first, hi - lo)], wo_recv.at[:, slot, :, pl.ds(lo, hi - lo)],
            ss, rs, at_dp(PLANE[n]),
        )

    def wo_blocks(n, lo, hi):
        return wo_recv.at[:, pl.ds(0, n), :, pl.ds(lo, hi - lo)]

    def by_parity(odd, f):
        pl.when(odd == 0)(lambda: f(0))
        pl.when(odd == 1)(lambda: f(128))

    def res_copy(n):
        first = pl.multiple_of(window_start(dp_of(PLANE[n])), 128)
        return remote(
            resf_v.at[:, pl.ds(first, WIN)], res_recv.at[dp], rb_s, rb_r, at_dp(PLANE[n])
        )

    def send_low(steps):
        for n in steps:
            to = dp_of(PLANE[n])
            by_parity(
                lax.rem(to, 2),
                lambda skip, n=n, to=to: wo_copy(
                    n, to, dp, skip, HALF, a2a_s.at[skip // 128], a2a_r.at[0]
                ).start(),
            )

    for n in range(15):
        wo_copy(n, dp_of(PLANE[n]), dp, HALF, WIN, a2a_s.at[2], a2a_r.at[1]).start()
    res_recv[dp] = resf_v[:, pl.ds(start, WIN)]
    w_copies = [local(8 + k, src, dst) for k, (src, dst) in enumerate(
        ((wg_hbm, wg_v), (wu_hbm, wu_v), (wd_hbm, wd_v)))]
    for copy in w_copies:
        copy.start()

    total = jnp.zeros((H, 1), F32)
    acc = jnp.zeros((H, LAT), F32)
    for i in range(NCHUNK):
        slot = lax.broadcasted_iota(jnp.int32, (H, CHUNK), 1) + i * CHUNK
        w = jnp.where(slot < length, jnp.exp(s_ref[i] - top), 0.0)
        total = total + jnp.sum(w, axis=1, keepdims=True)
        acc = acc + lax.dot_general(
            w.astype(BF16), cache_v[i, :LAT], (((1,), (1,)), ((), ())), preferred_element_type=F32
        )
    latent = acc / total

    for copy in small[4:]:
        copy.wait()
    lane = lax.broadcasted_iota(jnp.int32, (1, 128), 1)
    coef = jnp.zeros((1, 128), F32)
    for k in range(8):
        coef = jnp.where(jnp.bitwise_and(lane, 15) == ids_ref[0, k], rw_ref[0, k], coef)
    high = coef.astype(BF16).astype(F32)
    coef = jnp.where(lane < 16, high, jnp.where(lane < 32, coef - high, 0.0))

    lat_send[:, :, :LAT] = latent.reshape(8, 8, LAT).astype(BF16)
    lat_send[:, :, LAT:] = jnp.broadcast_to(coef.reshape(1, 1, 128), (8, 8, 128)).astype(BF16)

    def lat_copy(n):
        return remote(
            lat_send.at[t_of(LINE[n])], lat_recv.at[t], lat_s, lat_r, at_t(LINE[n])
        )

    for n in range(7):
        lat_copy(n).start()
    lat_recv[t] = lat_send[t]
    order_v[0, :64, :64] = onehot(
        64, lambda r: jnp.bitwise_and(r, 7) * 8 + jnp.right_shift(r, 3)
    )
    small[3].wait()
    gain = gain_ref[...]
    ig2_v[...] = 1.0 / (gain * gain)
    wuv_copy.wait()
    arrived(lat_recv.at[pl.ds(0, 7)], lat_r)

    lat = lat_recv[...].astype(F32).reshape(64, LAT + 128).astype(BF16)
    lat = dot(order_v[0, :64, :64], lat)
    pieces = [dot(lat[8 * h : 8 * h + 8, :LAT].astype(BF16), wuv_v[h]) for h in range(8)]
    pieces.append(lat[0:8, LAT:])
    vals_send[...] = jnp.concatenate(pieces, axis=1).astype(BF16)

    v1 = pos["x"] + core * (pos["y"] - pos["x"])
    v2 = pos["x"] + pos["y"] - v1

    def val_copy(k, i):
        here = vals_all.at[v2] if k else vals_all.at[v2, v1]
        dx = (1 - core) * i if k == 0 else core * i
        return remote(here, here, val_s.at[k], val_r.at[k], at_dp((dx, i - dx)))

    vals_all[v2, v1] = vals_send[...]
    for i in (2, 1, 3):
        val_copy(0, i).start()
    send_low(range(FIRST))
    def from_row(r, row_t):
        x, y = jnp.bitwise_and(jnp.right_shift(r, 2), 3), jnp.bitwise_and(r, 3)
        inner = x + core * (y - x)
        return (x + y - inner) * 32 + inner * 8 + row_t

    order_v[1] = onehot(128, lambda r: from_row(r, jnp.right_shift(r, 4)))
    order_v[2] = onehot(
        128,
        lambda r: from_row(
            r, jnp.bitwise_and(jnp.right_shift(r, 4), 3) * 2 + jnp.right_shift(r, 6)
        ),
    )
    bits = {"c": 6, "z": 4, "x": 2, "y": 0}
    for p in range(3):

        def source(r):
            src = jnp.left_shift(jnp.bitwise_xor(jnp.right_shift(r, 6), core), bits["c"])
            for a, shift in zip(ORDERS[p], (4, 2, 0)):
                src = src + jnp.left_shift(jnp.bitwise_and(jnp.right_shift(r, shift), 3), bits[a])
            return src

        order_v[3 + p] = onehot(128, source)
    arrived(vals_all.at[0, pl.ds(0, 3)], val_r.at[0])
    for i in (2, 1, 3):
        val_copy(1, i).start()
    send_low(range(FIRST, 15))
    for n in range(15):
        res_copy(n).start()
    own_wo.wait()
    arrived(wo_blocks(15, HALF, WIN), a2a_r.at[1])
    arrived(vals_all.at[pl.ds(0, 3)], val_r.at[1])

    vals_raw = vals_all[...].astype(F32).reshape(128, 1152).astype(BF16)
    vals = dot(order_v[1], vals_raw[:, : 8 * HD]).astype(BF16)

    def rs_copy(half, n):
        return remote(
            rs_send.at[half, t_of(LINE[n])], rs_recv.at[half, t],
            rs_s.at[half], rs_r.at[half], at_t(LINE[n]),
        )

    def project(half):
        part = jnp.zeros((128, HALF), F32)
        for h in range(8):
            w = wo_recv[h, :, :, half * HALF : half * HALF + HALF]
            part = part + dot(
                vals[:, h * HD : (h + 1) * HD], w.astype(F32).reshape(128, HALF).astype(BF16)
            )
        rs_send[half] = part.astype(BF16).reshape(8, 16, HALF)
        for n in range(7):
            rs_copy(half, n).start()
        rs_recv[half, t] = rs_send[half, t]

    project(1)

    coefs = dot(order_v[2], vals_raw[:, 8 * HD :])
    col = lax.broadcasted_iota(jnp.int32, (128, 128), 1)
    mine = (col == dp) | (col == dp + 16)
    coef_col = jnp.sum(jnp.where(mine, coefs, 0.0), axis=1, keepdims=True)

    by_parity(lax.rem(dp, 2), lambda skip: arrived(wo_blocks(15, skip, HALF), a2a_r.at[0]))
    project(0)

    def either(c, f):
        zero, one = f(0), f(1)
        return zero + c * (one - zero)

    def axis_of(j, c, k):
        return GATHER_ORDERS[TILE_ORDER[c][j]][k]

    def place(j, k, c):
        return either(c, lambda v: pos[axis_of(j, v, k)])

    def block(j, phase, c, i):
        at = [place(j, k, c) for k in (2, 1, 0)][: 3 - phase]
        at[-1] = lax.rem(at[-1] - i + 4, 4)
        return x_v.at[(j, c, *at)]

    def partner(j, k, i):
        return {
            name: either(core, lambda v, name=name: along(axis_of(j, v, k), i)[name])
            for name in ("dp", "tensor")
        }

    def spread(j):
        def go():
            here = x_v.at[j, core, place(j, 2, core), place(j, 1, core), place(j, 0, core)]
            for step in PLANE:
                target = {
                    name: either(
                        core,
                        lambda v, name=name: in_plane(axis_of(j, v, 0), axis_of(j, v, 1), step)[name],
                    )
                    for name in ("dp", "tensor")
                }
                remote(
                    here, here, ag_s.at[0 if j else 1], ag_r.at[j * 7 + step[1]], target
                ).start()

        if j == 0:
            pl.when(lax.rem(pos["y"], 2) == 0)(go)
        else:
            go()

    def rows_on(j, back):
        def go():
            n = 4 if back else 3
            arrived(x_v.at[0, 0, 0, 0, pl.ds(0, n)], ag_r.at[j * 7 + back])
            row = lax.rem(place(j, 1, core) - back + 4, 4)
            here = x_v.at[j, core, place(j, 2, core), row]
            for i in (2, 1, 3):
                remote(
                    here, here, ag_s.at[3 if j == 0 else 2], ag_r.at[j * 7 + 3 + i], partner(j, 2, i)
                ).start()

        if j == 0:
            pl.when(lax.rem(pos["y"] - back + 4, 2) == 0)(go)
        else:
            go()

    def to_sibling(j, i):
        there = block(j, 2, core, i)
        return remote(there, there, sib_s, sib_r, sibling)

    arrived(res_recv.at[pl.ds(0, 15)], rb_r)
    res = jnp.concatenate([res_recv[k] for k in range(16)], axis=0)
    st_send[...] = jnp.zeros_like(st_send)

    def send_half(half):
        arrived(rs_recv.at[half, pl.ds(0, 7)], rs_r.at[half])
        stream = res[:, half * HALF : half * HALF + HALF]
        for k in range(8):
            stream = stream + rs_recv[half, k].astype(F32)
        scaled = (stream * gain_ref[:, pl.ds(start + half * HALF, HALF)]).astype(BF16)
        for j in (1, 0):
            at = place(2 * half + j, 2, core), place(2 * half + j, 1, core), place(2 * half + j, 0, core)
            x_v[(2 * half + j, core, *at)] = scaled[:, 128 * j : 128 * j + 128]
            spread(2 * half + j)
        for j in range(2):
            st_send[pl.ds(2 * half + j, 16, stride=8), :] = stream[:, 128 * j : 128 * j + 128]

    send_half(1)
    send_half(0)

    st_recv[dp] = st_send[pl.ds(pl.multiple_of(dp * 8, 8), 8), :]

    def st_copy(n):
        there = pl.multiple_of(dp_of(PLANE[n]) * 8, 8)
        return remote(
            st_send.at[pl.ds(there, 8)], st_recv.at[dp], st_s, st_r, at_dp(PLANE[n])
        )

    for tiles in ((3, 2), (1, 0)):
        for back in (0, 1, 3, 2):
            for j in tiles:
                rows_on(j, back)
        for j in tiles:
            to_sibling(j, 0).start()

    for n in range(15):
        st_copy(n).start()

    def wo_sent(skip):
        for n, other in ((7, skip), (8, 128 - skip)):
            sent(wo_blocks(n, other, HALF), a2a_s.at[other // 128])

    by_parity(lax.rem(dp, 2), wo_sent)
    sent(wo_blocks(15, HALF, WIN), a2a_s.at[2])
    sent(res_recv.at[pl.ds(0, 15)], rb_s)
    sent(vals_all.at[0, pl.ds(0, 3)], val_s.at[0])
    sent(vals_all.at[pl.ds(0, 3)], val_s.at[1])
    sent(lat_recv.at[pl.ds(0, 7)], lat_s)
    for half in range(2):
        sent(rs_recv.at[half, pl.ds(0, 7)], rs_s.at[half])

    for i in (1, 3, 2):
        for j in (2, 3, 1, 0):
            arrived(x_v.at[0, 0, 0] if j else x_v.at[0, 0, 0, pl.ds(0, 2)], ag_r.at[j * 7 + 3 + i])
            to_sibling(j, i).start()
    arrived(x_v.at[:, 0], sib_r)
    for copy in w_copies:
        copy.wait()

    def tile_of(j, x, y):
        halves = []
        for c in range(2):
            at = {"x": x, "y": y, "z": slice(None)}
            i1, i2, i3 = (at[a] for a in GATHER_ORDERS[TILE_ORDER[c][j]])
            halves.append(x_v[j, c, i3, i2, i1].reshape(64, 128))
        return jnp.concatenate(halves, axis=0)

    def up_step(k, carry):
        g, u, sq = carry
        tiles = [tile_of(j, k, y) for y in range(4) for j in range(y % 2, 4)]
        for n, tile in enumerate(tiles):
            f = tile.astype(F32)
            sq = sq + f * f * ig2_v[:, pl.ds(pl.multiple_of(k * 1792 + n * 128, 128), 128)]
        x = jnp.concatenate(tiles, axis=1)
        rows = pl.ds(pl.multiple_of(k * 1792, 1792), 1792)
        return g + dot(x, wg_v[rows, :]), u + dot(x, wu_v[rows, :]), sq

    zero = jnp.zeros((128, FF), F32)
    g, u, sq = lax.fori_loop(
        0, 4, up_step, (zero, zero, jnp.zeros((128, 128), F32)), unroll=True
    )
    factor = lax.rsqrt(jnp.sum(sq, axis=1, keepdims=True) * (1.0 / D) + EPS)
    g = g * factor
    act = (g / (1.0 + jnp.exp(-g))) * (u * factor * coef_col)
    act = act.astype(BF16)

    acts = [dot(order_v[3 + p], act).astype(BF16) for p in range(3)]

    def core_copy(s):
        p, at, w = PIECES[s]
        cols = pl.ds(at, w)
        return remote(
            c_send.at[p, :, cols], c_recv.at[p, :, cols], cs_s, cs_r.at[s], sibling
        )

    def sum1(s, i):
        p, at, w = PIECES[s]
        axis = ORDERS[p][0]
        cols = pl.ds(at, w)
        return remote(
            p1.at[p, lax.rem(pos[axis] + i, 4), :, cols], p1r.at[p, i - 1, :, cols],
            p1_s, p1_r.at[p], along(axis, i),
        )

    def down(s):
        p, at, w = PIECES[s]
        first = PARTS[p][0] + at
        o = dot(acts[p], wd_v[:, first : first + w])
        d_own[p, :, at : at + w] = o[:64]
        c_send[p, :, at : at + w] = o[64:].astype(BF16)
        core_copy(s).start()

    def pair(s):
        p, at, w = PIECES[s]
        core_copy(s).wait_recv()
        o = d_own[p, :, at : at + w] + c_recv[p, :, at : at + w].astype(F32)
        p1[p, :, :, at : at + w] = o.reshape(4, 16, w).astype(BF16)
        for i in (2, 1, 3):
            sum1(s, i).start()

    def direct_copy(p, other, i):
        axis = ORDERS[p][0]
        target = along(axis, i)
        return remote(
            pd.at[p, other, lax.rem(pos[axis] + i, 4)], pdr.at[p, core * 4 + pos[axis]],
            pd_s, pd_r.at[p], crossed(target) if other else target,
        )

    def direct(p):
        first = PARTS[p][0]
        o = dot(acts[p], wd_v[:, first : first + DIRECT])
        pd[p] = o.reshape(2, 4, 16, DIRECT).astype(BF16)
        for other, i in ((1, 2), (0, 2), (1, 1), (1, 3), (0, 1), (0, 3), (1, 0)):
            direct_copy(p, other, i).start()
        pdr[p, core * 4 + pos[ORDERS[p][0]]] = pd[p, 0, pos[ORDERS[p][0]]]

    for p in range(3):
        direct(p)
    for s in range(3):
        down(s)
    for s in range(3):
        pair(s)

    def my_row(p):
        return pos[ORDERS[p][1]] * 4 + pos[ORDERS[p][2]]

    def row_copy(p, step):
        a, b = ORDERS[p][1], ORDERS[p][2]
        there = lax.rem(pos[a] + step[0], 4) * 4 + lax.rem(pos[b] + step[1], 4)
        return remote(
            q2.at[p, there], q2r.at[p, my_row(p)], p2_s, p2_r.at[p], in_plane(a, b, step)
        )

    q2f[...] = jnp.zeros_like(q2f)
    for p, (first, w) in enumerate(PARTS):
        arrived(pdr.at[p, pl.ds(0, 7)], pd_r.at[p])
        o = pdr[p, 0].astype(F32)
        for i in range(1, 8):
            o = o + pdr[p, i].astype(F32)
        arrived(p1r.at[p, :, :, pl.ds(DIRECT, w - DIRECT)], p1_r.at[p])
        rest = p1[p, pos[ORDERS[p][0]], :, DIRECT:w].astype(F32)
        for i in range(3):
            rest = rest + p1r[p, i, :, DIRECT:w].astype(F32)
        o = jnp.concatenate([o, rest], axis=1)
        for j in range(w // 128):
            q2f[pl.ds(j, 16, stride=SPAN), :] = o[:, 128 * j : 128 * j + 128]
        q2[p] = q2f[...].reshape(16, SPAN, 128).astype(BF16)
        for step in PLANE:
            row_copy(p, step).start()
        q2r[p, my_row(p)] = q2[p, my_row(p)]

    arrived(st_recv.at[pl.ds(0, 15)], st_r)
    sent(st_recv.at[pl.ds(0, 15)], st_s)
    for k in range(8):
        mix_v[7 * k : 7 * k + 4, :] = st_recv[2 * k, 0:4, :]
        mix_v[7 * k + 4 : 7 * k + 7, :] = st_recv[2 * k + 1, 1:4, :]

    sent(q2f.at[pl.ds(0, 360)], ag_s.at[0])

    @pl.when(lax.rem(pos["y"], 2) == 0)
    def _():
        sent(q2f.at[pl.ds(0, 120)], ag_s.at[1])

    sent(x_v.at[pl.ds(0, 3), 0, pl.ds(0, 3)], ag_s.at[2])
    sent(x_v.at[pl.ds(0, 2), 0, 0, pl.ds(0, 3)], ag_s.at[3])
    sent(x_v.at[:, 0], sib_s)
    sent(wd_v.at[pl.ds(0, 64), pl.ds(0, D - 3 * DIRECT)], cs_s)
    sent(wd_v.at[pl.ds(0, 48), pl.ds(0, D - 3 * DIRECT)], p1_s)
    sent(pdr.at[:, pl.ds(0, 7)], pd_s)

    for p, (first, w) in enumerate(PARTS):
        arrived(q2r.at[p, pl.ds(0, 15)], p2_r.at[p])
        o = q2r[p, 0].astype(F32)
        for i in range(1, 16):
            o = o + q2r[p, i].astype(F32)
        tiles = slice(first // 128, (first + w) // 128)
        mix_v[tiles, :] = mix_v[tiles, :] + o[: w // 128]
    out_ref[...] = mix_v[...].astype(BF16)
    sent(q2r.at[:, pl.ds(0, 15)], p2_s)


def on_device(
    residual, query_latent, latent_cache, lengths, w_uv, w_o, norm_gain, expert_ids, route_weights,
    w_gate, w_up, w_down,
):
    dma = pltpu.SemaphoreType.DMA
    vmem = pl.BlockSpec(memory_space=pltpu.VMEM)
    hbm = pl.BlockSpec(memory_space=pl.ANY)
    wide = max(w for _, w in PARTS)
    out = pl.pallas_call(
        layer,
        out_shape=jax.ShapeDtypeStruct((D // 128, 128), BF16),
        in_specs=[hbm] * 12,
        out_specs=vmem,
        scratch_shapes=[
            pltpu.SMEM((1,), jnp.int32),
            pltpu.SMEM((1, 8), jnp.int32),
            pltpu.SMEM((1, 8), F32),
            pltpu.VMEM((1, D), BF16),
            pltpu.VMEM((H, CW), BF16),
            pltpu.VMEM((1, D), F32),
            pltpu.VMEM((NCHUNK, CW, CHUNK), BF16),
            pltpu.VMEM((8, LAT, HD), BF16),
            pltpu.VMEM((D, FF), BF16),
            pltpu.VMEM((D, FF), BF16),
            pltpu.VMEM((FF, D), BF16),
            pltpu.VMEM((NCHUNK, H, CHUNK), F32),
            pltpu.VMEM((1, D), F32),
            pltpu.VMEM((16, 1, WIN), F32),
            pltpu.VMEM((8, 16, 8, WIN), BF16),
            pltpu.VMEM((8, 8, LAT + 128), BF16),
            pltpu.VMEM((8, 8, LAT + 128), BF16),
            pltpu.VMEM((8, 1152), BF16),
            pltpu.VMEM((4, 4, 8, 1152), BF16),
            pltpu.VMEM((2, 8, 16, HALF), BF16),
            pltpu.VMEM((2, 8, 16, HALF), BF16),
            pltpu.VMEM((128, 128), F32),
            pltpu.VMEM((16, 8, 128), F32),
            pltpu.VMEM((4, 2, 4, 4, 4, 16, 128), BF16),
            pltpu.VMEM((1, D), F32),
            pltpu.VMEM((3, 64, wide), F32),
            pltpu.VMEM((3, 64, wide), BF16),
            pltpu.VMEM((3, 64, wide), BF16),
            pltpu.VMEM((3, 4, 16, wide), BF16),
            pltpu.VMEM((3, 3, 16, wide), BF16),
            pltpu.VMEM((16 * SPAN, 128), F32),
            pltpu.VMEM((3, 16, SPAN, 128), BF16),
            pltpu.VMEM((3, 16, SPAN, 128), BF16),
            pltpu.VMEM((D // 128, 128), F32),
            pltpu.VMEM((6, 128, 128), BF16),
            pltpu.VMEM((3, 2, 4, 16, DIRECT), BF16),
            pltpu.VMEM((3, 8, 16, DIRECT), BF16),
            dma((NCHUNK + 11,)),
            dma((3,)), dma((2,)), dma, dma, dma, dma, dma((2,)), dma((2,)),
            dma((2,)), dma((2,)), dma, dma, dma((4,)), dma((28,)), dma, dma,
            dma, dma((3,)), dma, dma((3,)), dma, dma((3,)), dma, dma((3,)),
        ],
        compiler_params=pltpu.CompilerParams(
            collective_id=0, has_side_effects=True, vmem_limit_bytes=56 * 1024 * 1024
        ),
    )(
        lengths, expert_ids, route_weights, residual, query_latent, norm_gain.reshape(1, D),
        latent_cache.swapaxes(1, 2), w_uv, w_o, w_gate.reshape(D, FF), w_up.reshape(D, FF), w_down.reshape(FF, D),
    )
    return out.reshape(1, D)


def solution(mesh):
    return jax.shard_map(
        on_device,
        mesh=mesh,
        in_specs=(
            P(("dp", "tensor"), None),
            P(("dp", "tensor"), None, None),
            P(("dp", "tensor"), None, None),
            P(("dp", "tensor")),
            P("tensor", None, None),
            P("tensor", "dp", None),
            P(),
            P(("dp", "tensor"), None),
            P(("dp", "tensor"), None),
            P("dp", None, "tensor"),
            P("dp", None, "tensor"),
            P("dp", "tensor", None),
        ),
        out_specs=P(("dp", "tensor"), None),
        check_vma=False,
    )
```

```python
import jax
import jax.numpy as jnp
from jax import lax
from jax.experimental import pallas as pl
from jax.experimental.pallas import tpu as pltpu
from jax.sharding import PartitionSpec as P

MESH = pl.DeviceIdType.MESH
F32 = jnp.float32
BF16 = jnp.bfloat16

CTX, CW, LAT = 4096, 576, 512
D, H, HD, FF = 7168, 64, 128, 256
CHUNK = 1024
NCHUNK = CTX // CHUNK
WIN = 512
HALF = 256
SCALE = 192 ** (-0.5)
EPS = 1e-06
MASKED = -1e30
PARTS = ((0, 2432), (2432, 2432), (4864, 2304))
DIRECT = 768
PIECES = ((0, 768, 1664), (1, 768, 1664), (2, 768, 1536))
ORDERS = (("z", "y", "x"), ("x", "z", "y"), ("y", "x", "z"))
GATHER_ORDERS = (("z", "y", "x"), ("x", "z", "y"), ("x", "y", "z"))
TILE_ORDER = ((2, 0, 0, 1), (0, 1, 2, 2))
SPAN = 24
PLANE = (
    (2, 2), (2, 1), (1, 2), (2, 3), (3, 2), (2, 0), (0, 2), (1, 1), (3, 3), (1, 3), (3, 1),
    (1, 0), (0, 1), (3, 0), (0, 3),
)
FIRST = 5
LINE = ((2, 1), (2, 0), (1, 1), (3, 1), (1, 0), (3, 0), (0, 1))


def window_start(dp):
    return (dp // 2) * 896 + (dp % 2) * 384


def onehot(n, source):
    row = lax.broadcasted_iota(jnp.int32, (n, n), 0)
    col = lax.broadcasted_iota(jnp.int32, (n, n), 1)
    return jnp.where(col == source(row), 1.0, 0.0).astype(BF16)


def dot(a, b):
    return jnp.dot(a, b, preferred_element_type=F32)


def layer(
    len_hbm, ids_hbm, rw_hbm, res_hbm, q_hbm, gain_hbm,
    cache_hbm, wuv_hbm, wo_hbm, wg_hbm, wu_hbm, wd_hbm,
    out_ref,
    len_ref, ids_ref, rw_ref, res_ref, q_ref, gain_ref,
    cache_v, wuv_v, wg_v, wu_v, wd_v,
    s_ref, resf_v, res_recv, wo_recv, lat_send, lat_recv, vals_send, vals_all,
    rs_send, rs_recv, st_send, st_recv, x_v, ig2_v,
    d_own, c_send, c_recv, p1, p1r, q2f, q2, q2r, mix_v, order_v, pd, pdr,
    local_sem, a2a_s, a2a_r, rb_s, rb_r, lat_s, lat_r, val_s, val_r,
    rs_s, rs_r, st_s, st_r, ag_s, ag_r, sib_s, sib_r,
    cs_s, cs_r, p1_s, p1_r, p2_s, p2_r, pd_s, pd_r,
):
    dp = lax.axis_index("dp")
    t = lax.axis_index("tensor")
    pos = {"x": dp // 4, "y": dp % 4, "z": t // 2, "c": t % 2}
    core = pos["c"]

    def dp_of(step):
        return lax.rem(pos["x"] + step[0], 4) * 4 + lax.rem(pos["y"] + step[1], 4)

    def t_of(step):
        return lax.rem(pos["z"] + step[0], 4) * 2 + lax.rem(core + step[1], 2)

    def at_dp(step):
        return {"dp": dp_of(step), "tensor": t}

    def at_t(step):
        return {"dp": dp, "tensor": t_of(step)}

    def along(axis, i):
        new = dict(pos)
        new[axis] = lax.rem(pos[axis] + i, 4)
        return {"dp": new["x"] * 4 + new["y"], "tensor": new["z"] * 2 + new["c"]}

    def in_plane(a, b, step):
        new = dict(pos)
        new[a] = lax.rem(pos[a] + step[0], 4)
        new[b] = lax.rem(pos[b] + step[1], 4)
        return {"dp": new["x"] * 4 + new["y"], "tensor": new["z"] * 2 + new["c"]}

    def crossed(device):
        return {"dp": device["dp"], "tensor": device["tensor"] + 1 - 2 * core}

    sibling = {"dp": dp, "tensor": pos["z"] * 2 + (1 - core)}

    def remote(src, dst, ss, rs, dev):
        return pltpu.make_async_remote_copy(
            src_ref=src, dst_ref=dst, send_sem=ss, recv_sem=rs, device_id=dev, device_id_type=MESH
        )

    def sent(ref, sem):
        remote(ref, ref, sem, sem, sibling).wait_send()

    def arrived(ref, sem):
        remote(ref, ref, sem, sem, sibling).wait_recv()

    def cache_copy(i):
        return pltpu.make_async_copy(
            cache_hbm.at[0, :, pl.ds(pl.multiple_of(i * CHUNK, CHUNK), CHUNK)],
            cache_v.at[i],
            local_sem.at[i],
        )

    def local(n, src, dst):
        return pltpu.make_async_copy(src, dst, local_sem.at[NCHUNK + n])

    small = [
        local(0, q_hbm.at[0], q_ref), local(1, len_hbm, len_ref), local(2, res_hbm, res_ref),
        local(3, gain_hbm, gain_ref), local(4, ids_hbm, ids_ref), local(5, rw_hbm, rw_ref),
    ]
    small[0].start()
    small[1].start()
    cache_copy(0).start()
    small[2].start()
    for i in range(1, NCHUNK):
        cache_copy(i).start()
    for copy in small[3:]:
        copy.start()
    barrier = pltpu.get_barrier_semaphore()
    peers = [at_dp(step) for step in PLANE] + [at_t(step) for step in LINE]
    for d in (1, 2, 3):
        for e in (1, 2, 3):
            peers += [in_plane("x", "z", (d, e)), in_plane("y", "z", (d, e))]
        peers += [crossed(along("x", d)), crossed(along("y", d))]
    for peer in peers:
        pl.semaphore_signal(barrier, inc=1, device_id=peer, device_id_type=MESH)

    start = pl.multiple_of(window_start(dp), 128)
    own_wo = local(6, wo_hbm.at[:, :, pl.ds(start, WIN)], wo_recv.at[:, dp])
    own_wo.start()
    wuv_copy = local(7, wuv_hbm, wuv_v)
    wuv_copy.start()

    for copy in small[:2]:
        copy.wait()
    length = len_ref[0]
    q = q_ref[...]

    def score(i, top):
        cache_copy(i).wait()
        s = dot(q, cache_v[i]) * SCALE
        slot = lax.broadcasted_iota(jnp.int32, (H, CHUNK), 1) + i * CHUNK
        s = jnp.where(slot < length, s, MASKED)
        s_ref[i] = s
        return jnp.maximum(top, jnp.max(s, axis=1, keepdims=True))

    top = jnp.full((H, 1), MASKED, F32)
    for i in range(NCHUNK):
        top = score(i, top)

    small[2].wait()
    resf_v[...] = res_ref[...].astype(F32)
    pl.semaphore_wait(barrier, 46)

    def wo_copy(n, src_dp, slot, lo, hi, ss, rs):
        first = pl.multiple_of(window_start(src_dp) + lo, 128)
        return remote(
            wo_hbm.at[:, :, pl.ds(first, hi - lo)], wo_recv.at[:, slot, :, pl.ds(lo, hi - lo)],
            ss, rs, at_dp(PLANE[n]),
        )

    def wo_blocks(n, lo, hi):
        return wo_recv.at[:, pl.ds(0, n), :, pl.ds(lo, hi - lo)]

    def by_parity(odd, f):
        pl.when(odd == 0)(lambda: f(0))
        pl.when(odd == 1)(lambda: f(128))

    def res_copy(n):
        first = pl.multiple_of(window_start(dp_of(PLANE[n])), 128)
        return remote(
            resf_v.at[:, pl.ds(first, WIN)], res_recv.at[dp], rb_s, rb_r, at_dp(PLANE[n])
        )

    def send_low(steps):
        for n in steps:
            to = dp_of(PLANE[n])
            by_parity(
                lax.rem(to, 2),
                lambda skip, n=n, to=to: wo_copy(
                    n, to, dp, skip, HALF, a2a_s.at[skip // 128], a2a_r.at[0]
                ).start(),
            )

    for n in range(15):
        wo_copy(n, dp_of(PLANE[n]), dp, HALF, WIN, a2a_s.at[2], a2a_r.at[1]).start()
    res_recv[dp] = resf_v[:, pl.ds(start, WIN)]
    w_copies = [local(8 + k, src, dst) for k, (src, dst) in enumerate(
        ((wg_hbm, wg_v), (wu_hbm, wu_v), (wd_hbm, wd_v)))]
    for copy in w_copies:
        copy.start()

    total = jnp.zeros((H, 1), F32)
    acc = jnp.zeros((H, LAT), F32)
    for i in range(NCHUNK):
        slot = lax.broadcasted_iota(jnp.int32, (H, CHUNK), 1) + i * CHUNK
        w = jnp.where(slot < length, jnp.exp(s_ref[i] - top), 0.0)
        total = total + jnp.sum(w, axis=1, keepdims=True)
        acc = acc + lax.dot_general(
            w.astype(BF16), cache_v[i, :LAT], (((1,), (1,)), ((), ())), preferred_element_type=F32
        )
    latent = acc / total

    for copy in small[4:]:
        copy.wait()
    lane = lax.broadcasted_iota(jnp.int32, (1, 128), 1)
    coef = jnp.zeros((1, 128), F32)
    for k in range(8):
        coef = jnp.where(jnp.bitwise_and(lane, 15) == ids_ref[0, k], rw_ref[0, k], coef)
    high = coef.astype(BF16).astype(F32)
    coef = jnp.where(lane < 16, high, jnp.where(lane < 32, coef - high, 0.0))

    lat_send[:, :, :LAT] = latent.reshape(8, 8, LAT).astype(BF16)
    lat_send[:, :, LAT:] = jnp.broadcast_to(coef.reshape(1, 1, 128), (8, 8, 128)).astype(BF16)

    def lat_copy(n):
        return remote(
            lat_send.at[t_of(LINE[n])], lat_recv.at[t], lat_s, lat_r, at_t(LINE[n])
        )

    for n in range(7):
        lat_copy(n).start()
    lat_recv[t] = lat_send[t]
    order_v[0, :64, :64] = onehot(
        64, lambda r: jnp.bitwise_and(r, 7) * 8 + jnp.right_shift(r, 3)
    )
    small[3].wait()
    gain = gain_ref[...]
    ig2_v[...] = 1.0 / (gain * gain)
    wuv_copy.wait()
    arrived(lat_recv.at[pl.ds(0, 7)], lat_r)

    lat = lat_recv[...].astype(F32).reshape(64, LAT + 128).astype(BF16)
    lat = dot(order_v[0, :64, :64], lat)
    pieces = [dot(lat[8 * h : 8 * h + 8, :LAT].astype(BF16), wuv_v[h]) for h in range(8)]
    pieces.append(lat[0:8, LAT:])
    vals_send[...] = jnp.concatenate(pieces, axis=1).astype(BF16)

    v1 = pos["x"] + core * (pos["y"] - pos["x"])
    v2 = pos["x"] + pos["y"] - v1

    def val_copy(k, i):
        here = vals_all.at[v2] if k else vals_all.at[v2, v1]
        dx = (1 - core) * i if k == 0 else core * i
        return remote(here, here, val_s.at[k], val_r.at[k], at_dp((dx, i - dx)))

    vals_all[v2, v1] = vals_send[...]
    for i in (2, 1, 3):
        val_copy(0, i).start()
    send_low(range(FIRST))
    def from_row(r, row_t):
        x, y = jnp.bitwise_and(jnp.right_shift(r, 2), 3), jnp.bitwise_and(r, 3)
        inner = x + core * (y - x)
        return (x + y - inner) * 32 + inner * 8 + row_t

    order_v[1] = onehot(128, lambda r: from_row(r, jnp.right_shift(r, 4)))
    order_v[2] = onehot(
        128,
        lambda r: from_row(
            r, jnp.bitwise_and(jnp.right_shift(r, 4), 3) * 2 + jnp.right_shift(r, 6)
        ),
    )
    bits = {"c": 6, "z": 4, "x": 2, "y": 0}
    for p in range(3):

        def source(r):
            src = jnp.left_shift(jnp.bitwise_xor(jnp.right_shift(r, 6), core), bits["c"])
            for a, shift in zip(ORDERS[p], (4, 2, 0)):
                src = src + jnp.left_shift(jnp.bitwise_and(jnp.right_shift(r, shift), 3), bits[a])
            return src

        order_v[3 + p] = onehot(128, source)
    arrived(vals_all.at[0, pl.ds(0, 3)], val_r.at[0])
    for i in (2, 1, 3):
        val_copy(1, i).start()
    send_low(range(FIRST, 15))
    for n in range(15):
        res_copy(n).start()
    own_wo.wait()
    arrived(wo_blocks(15, HALF, WIN), a2a_r.at[1])
    arrived(vals_all.at[pl.ds(0, 3)], val_r.at[1])

    vals_raw = vals_all[...].astype(F32).reshape(128, 1152).astype(BF16)
    vals = dot(order_v[1], vals_raw[:, : 8 * HD]).astype(BF16)

    def rs_copy(half, n):
        return remote(
            rs_send.at[half, t_of(LINE[n])], rs_recv.at[half, t],
            rs_s.at[half], rs_r.at[half], at_t(LINE[n]),
        )

    def project(half):
        part = jnp.zeros((128, HALF), F32)
        for h in range(8):
            w = wo_recv[h, :, :, half * HALF : half * HALF + HALF]
            part = part + dot(
                vals[:, h * HD : (h + 1) * HD], w.astype(F32).reshape(128, HALF).astype(BF16)
            )
        rs_send[half] = part.astype(BF16).reshape(8, 16, HALF)
        for n in range(7):
            rs_copy(half, n).start()
        rs_recv[half, t] = rs_send[half, t]

    project(1)

    coefs = dot(order_v[2], vals_raw[:, 8 * HD :])
    col = lax.broadcasted_iota(jnp.int32, (128, 128), 1)
    mine = (col == dp) | (col == dp + 16)
    coef_col = jnp.sum(jnp.where(mine, coefs, 0.0), axis=1, keepdims=True)

    by_parity(lax.rem(dp, 2), lambda skip: arrived(wo_blocks(15, skip, HALF), a2a_r.at[0]))
    project(0)

    def either(c, f):
        zero, one = f(0), f(1)
        return zero + c * (one - zero)

    def axis_of(j, c, k):
        return GATHER_ORDERS[TILE_ORDER[c][j]][k]

    def place(j, k, c):
        return either(c, lambda v: pos[axis_of(j, v, k)])

    def block(j, phase, c, i):
        at = [place(j, k, c) for k in (2, 1, 0)][: 3 - phase]
        at[-1] = lax.rem(at[-1] - i + 4, 4)
        return x_v.at[(j, c, *at)]

    def partner(j, k, i):
        return {
            name: either(core, lambda v, name=name: along(axis_of(j, v, k), i)[name])
            for name in ("dp", "tensor")
        }

    def spread(j):
        def go():
            here = x_v.at[j, core, place(j, 2, core), place(j, 1, core), place(j, 0, core)]
            for step in PLANE:
                target = {
                    name: either(
                        core,
                        lambda v, name=name: in_plane(axis_of(j, v, 0), axis_of(j, v, 1), step)[name],
                    )
                    for name in ("dp", "tensor")
                }
                remote(
                    here, here, ag_s.at[0 if j else 1], ag_r.at[j * 4 + step[1]], target
                ).start()

        if j == 0:
            pl.when(lax.rem(pos["y"], 2) == 0)(go)
        else:
            go()

    def rows_on(j, back):
        def go():
            n = 4 if back else 3
            arrived(x_v.at[0, 0, 0, 0, pl.ds(0, n)], ag_r.at[j * 4 + back])
            row = lax.rem(place(j, 1, core) - back + 4, 4)
            here = x_v.at[j, core, place(j, 2, core), row]
            for i in (2, 1, 3):
                remote(
                    here, here, ag_s.at[3 if j == 0 else 2], ag_r.at[16 + (j // 2) * 3 + i - 1], partner(j, 2, i)
                ).start()

        if j == 0:
            pl.when(lax.rem(pos["y"] - back + 4, 2) == 0)(go)
        else:
            go()

    def to_sibling(j, i):
        there = block(j, 2, core, i)
        return remote(there, there, sib_s, sib_r, sibling)

    arrived(res_recv.at[pl.ds(0, 15)], rb_r)
    res = jnp.concatenate([res_recv[k] for k in range(16)], axis=0)
    st_send[...] = jnp.zeros_like(st_send)

    def send_half(half):
        arrived(rs_recv.at[half, pl.ds(0, 7)], rs_r.at[half])
        stream = res[:, half * HALF : half * HALF + HALF]
        for k in range(8):
            stream = stream + rs_recv[half, k].astype(F32)
        scaled = (stream * gain_ref[:, pl.ds(start + half * HALF, HALF)]).astype(BF16)
        for j in (1, 0):
            at = place(2 * half + j, 2, core), place(2 * half + j, 1, core), place(2 * half + j, 0, core)
            x_v[(2 * half + j, core, *at)] = scaled[:, 128 * j : 128 * j + 128]
            spread(2 * half + j)
        for j in range(2):
            st_send[pl.ds(2 * half + j, 16, stride=8), :] = stream[:, 128 * j : 128 * j + 128]

    send_half(1)
    send_half(0)

    st_recv[dp] = st_send[pl.ds(pl.multiple_of(dp * 8, 8), 8), :]

    def st_copy(n):
        there = pl.multiple_of(dp_of(PLANE[n]) * 8, 8)
        return remote(
            st_send.at[pl.ds(there, 8)], st_recv.at[dp], st_s, st_r, at_dp(PLANE[n])
        )

    for tiles in ((3, 2), (1, 0)):
        for back in (0, 1, 3, 2):
            for j in tiles:
                rows_on(j, back)
        for j in tiles:
            to_sibling(j, 0).start()

    for n in range(15):
        st_copy(n).start()

    def wo_sent(skip):
        for n, other in ((7, skip), (8, 128 - skip)):
            sent(wo_blocks(n, other, HALF), a2a_s.at[other // 128])

    by_parity(lax.rem(dp, 2), wo_sent)
    sent(wo_blocks(15, HALF, WIN), a2a_s.at[2])
    sent(res_recv.at[pl.ds(0, 15)], rb_s)
    sent(vals_all.at[0, pl.ds(0, 3)], val_s.at[0])
    sent(vals_all.at[pl.ds(0, 3)], val_s.at[1])
    sent(lat_recv.at[pl.ds(0, 7)], lat_s)
    for half in range(2):
        sent(rs_recv.at[half, pl.ds(0, 7)], rs_s.at[half])

    for i in (1, 3, 2):
        for half, both in ((1, x_v.at[pl.ds(0, 2), 0, 0]), (0, x_v.at[pl.ds(0, 3), 0, 0, pl.ds(0, 2)])):
            arrived(both, ag_r.at[16 + half * 3 + i - 1])
            for j in (2 * half + 1, 2 * half):
                to_sibling(j, i).start()
    arrived(x_v.at[:, 0], sib_r)
    for copy in w_copies:
        copy.wait()

    def tile_of(j, x, y):
        halves = []
        for c in range(2):
            at = {"x": x, "y": y, "z": slice(None)}
            i1, i2, i3 = (at[a] for a in GATHER_ORDERS[TILE_ORDER[c][j]])
            halves.append(x_v[j, c, i3, i2, i1].reshape(64, 128))
        return jnp.concatenate(halves, axis=0)

    def up_step(k, carry):
        g, u, sq = carry
        tiles = [tile_of(j, k, y) for y in range(4) for j in range(y % 2, 4)]
        for n, tile in enumerate(tiles):
            f = tile.astype(F32)
            sq = sq + f * f * ig2_v[:, pl.ds(pl.multiple_of(k * 1792 + n * 128, 128), 128)]
        x = jnp.concatenate(tiles, axis=1)
        rows = pl.ds(pl.multiple_of(k * 1792, 1792), 1792)
        return g + dot(x, wg_v[rows, :]), u + dot(x, wu_v[rows, :]), sq

    zero = jnp.zeros((128, FF), F32)
    g, u, sq = lax.fori_loop(
        0, 4, up_step, (zero, zero, jnp.zeros((128, 128), F32)), unroll=True
    )
    factor = lax.rsqrt(jnp.sum(sq, axis=1, keepdims=True) * (1.0 / D) + EPS)
    g = g * factor
    act = (g / (1.0 + jnp.exp(-g))) * (u * factor * coef_col)
    act = act.astype(BF16)

    acts = [dot(order_v[3 + p], act).astype(BF16) for p in range(3)]

    def core_copy(s):
        p, at, w = PIECES[s]
        cols = pl.ds(at, w)
        return remote(
            c_send.at[p, :, cols], c_recv.at[p, :, cols], cs_s, cs_r.at[s], sibling
        )

    def sum1(s, i):
        p, at, w = PIECES[s]
        axis = ORDERS[p][0]
        cols = pl.ds(at, w)
        return remote(
            p1.at[p, lax.rem(pos[axis] + i, 4), :, cols], p1r.at[p, i - 1, :, cols],
            p1_s, p1_r.at[p], along(axis, i),
        )

    def down(s):
        p, at, w = PIECES[s]
        first = PARTS[p][0] + at
        o = dot(acts[p], wd_v[:, first : first + w])
        d_own[p, :, at : at + w] = o[:64]
        c_send[p, :, at : at + w] = o[64:].astype(BF16)
        core_copy(s).start()

    def pair(s):
        p, at, w = PIECES[s]
        core_copy(s).wait_recv()
        o = d_own[p, :, at : at + w] + c_recv[p, :, at : at + w].astype(F32)
        p1[p, :, :, at : at + w] = o.reshape(4, 16, w).astype(BF16)
        for i in (2, 1, 3):
            sum1(s, i).start()

    def direct_copy(p, other, i):
        axis = ORDERS[p][0]
        target = along(axis, i)
        return remote(
            pd.at[p, other, lax.rem(pos[axis] + i, 4)], pdr.at[p, core * 4 + pos[axis]],
            pd_s, pd_r.at[p], crossed(target) if other else target,
        )

    def direct(p):
        first = PARTS[p][0]
        o = dot(acts[p], wd_v[:, first : first + DIRECT])
        pd[p] = o.reshape(2, 4, 16, DIRECT).astype(BF16)
        for other, i in ((1, 2), (0, 2), (1, 1), (1, 3), (0, 1), (0, 3), (1, 0)):
            direct_copy(p, other, i).start()
        pdr[p, core * 4 + pos[ORDERS[p][0]]] = pd[p, 0, pos[ORDERS[p][0]]]

    for p in range(3):
        direct(p)
    for s in range(3):
        down(s)
    for s in range(3):
        pair(s)

    def my_row(p):
        return pos[ORDERS[p][1]] * 4 + pos[ORDERS[p][2]]

    def row_copy(p, step):
        a, b = ORDERS[p][1], ORDERS[p][2]
        there = lax.rem(pos[a] + step[0], 4) * 4 + lax.rem(pos[b] + step[1], 4)
        return remote(
            q2.at[p, there], q2r.at[p, my_row(p)], p2_s, p2_r.at[p], in_plane(a, b, step)
        )

    q2f[...] = jnp.zeros_like(q2f)
    for p, (first, w) in enumerate(PARTS):
        arrived(pdr.at[p, pl.ds(0, 7)], pd_r.at[p])
        o = pdr[p, 0].astype(F32)
        for i in range(1, 8):
            o = o + pdr[p, i].astype(F32)
        arrived(p1r.at[p, :, :, pl.ds(DIRECT, w - DIRECT)], p1_r.at[p])
        rest = p1[p, pos[ORDERS[p][0]], :, DIRECT:w].astype(F32)
        for i in range(3):
            rest = rest + p1r[p, i, :, DIRECT:w].astype(F32)
        o = jnp.concatenate([o, rest], axis=1)
        for j in range(w // 128):
            q2f[pl.ds(j, 16, stride=SPAN), :] = o[:, 128 * j : 128 * j + 128]
        q2[p] = q2f[...].reshape(16, SPAN, 128).astype(BF16)
        for step in PLANE:
            row_copy(p, step).start()
        q2r[p, my_row(p)] = q2[p, my_row(p)]

    arrived(st_recv.at[pl.ds(0, 15)], st_r)
    sent(st_recv.at[pl.ds(0, 15)], st_s)
    for k in range(8):
        mix_v[7 * k : 7 * k + 4, :] = st_recv[2 * k, 0:4, :]
        mix_v[7 * k + 4 : 7 * k + 7, :] = st_recv[2 * k + 1, 1:4, :]

    sent(q2f.at[pl.ds(0, 360)], ag_s.at[0])

    @pl.when(lax.rem(pos["y"], 2) == 0)
    def _():
        sent(q2f.at[pl.ds(0, 120)], ag_s.at[1])

    sent(x_v.at[pl.ds(0, 3), 0, pl.ds(0, 3)], ag_s.at[2])
    sent(x_v.at[pl.ds(0, 2), 0, 0, pl.ds(0, 3)], ag_s.at[3])
    sent(x_v.at[:, 0], sib_s)
    sent(wd_v.at[pl.ds(0, 64), pl.ds(0, D - 3 * DIRECT)], cs_s)
    sent(wd_v.at[pl.ds(0, 48), pl.ds(0, D - 3 * DIRECT)], p1_s)
    sent(pdr.at[:, pl.ds(0, 7)], pd_s)

    for p, (first, w) in enumerate(PARTS):
        arrived(q2r.at[p, pl.ds(0, 15)], p2_r.at[p])
        o = q2r[p, 0].astype(F32)
        for i in range(1, 16):
            o = o + q2r[p, i].astype(F32)
        tiles = slice(first // 128, (first + w) // 128)
        mix_v[tiles, :] = mix_v[tiles, :] + o[: w // 128]
    out_ref[...] = mix_v[...].astype(BF16)
    sent(q2r.at[:, pl.ds(0, 15)], p2_s)


def on_device(
    residual, query_latent, latent_cache, lengths, w_uv, w_o, norm_gain, expert_ids, route_weights,
    w_gate, w_up, w_down,
):
    dma = pltpu.SemaphoreType.DMA
    vmem = pl.BlockSpec(memory_space=pltpu.VMEM)
    hbm = pl.BlockSpec(memory_space=pl.ANY)
    wide = max(w for _, w in PARTS)
    out = pl.pallas_call(
        layer,
        out_shape=jax.ShapeDtypeStruct((D // 128, 128), BF16),
        in_specs=[hbm] * 12,
        out_specs=vmem,
        scratch_shapes=[
            pltpu.SMEM((1,), jnp.int32),
            pltpu.SMEM((1, 8), jnp.int32),
            pltpu.SMEM((1, 8), F32),
            pltpu.VMEM((1, D), BF16),
            pltpu.VMEM((H, CW), BF16),
            pltpu.VMEM((1, D), F32),
            pltpu.VMEM((NCHUNK, CW, CHUNK), BF16),
            pltpu.VMEM((8, LAT, HD), BF16),
            pltpu.VMEM((D, FF), BF16),
            pltpu.VMEM((D, FF), BF16),
            pltpu.VMEM((FF, D), BF16),
            pltpu.VMEM((NCHUNK, H, CHUNK), F32),
            pltpu.VMEM((1, D), F32),
            pltpu.VMEM((16, 1, WIN), F32),
            pltpu.VMEM((8, 16, 8, WIN), BF16),
            pltpu.VMEM((8, 8, LAT + 128), BF16),
            pltpu.VMEM((8, 8, LAT + 128), BF16),
            pltpu.VMEM((8, 1152), BF16),
            pltpu.VMEM((4, 4, 8, 1152), BF16),
            pltpu.VMEM((2, 8, 16, HALF), BF16),
            pltpu.VMEM((2, 8, 16, HALF), BF16),
            pltpu.VMEM((128, 128), F32),
            pltpu.VMEM((16, 8, 128), F32),
            pltpu.VMEM((4, 2, 4, 4, 4, 16, 128), BF16),
            pltpu.VMEM((1, D), F32),
            pltpu.VMEM((3, 64, wide), F32),
            pltpu.VMEM((3, 64, wide), BF16),
            pltpu.VMEM((3, 64, wide), BF16),
            pltpu.VMEM((3, 4, 16, wide), BF16),
            pltpu.VMEM((3, 3, 16, wide), BF16),
            pltpu.VMEM((16 * SPAN, 128), F32),
            pltpu.VMEM((3, 16, SPAN, 128), BF16),
            pltpu.VMEM((3, 16, SPAN, 128), BF16),
            pltpu.VMEM((D // 128, 128), F32),
            pltpu.VMEM((6, 128, 128), BF16),
            pltpu.VMEM((3, 2, 4, 16, DIRECT), BF16),
            pltpu.VMEM((3, 8, 16, DIRECT), BF16),
            dma((NCHUNK + 11,)),
            dma((3,)), dma((2,)), dma, dma, dma, dma, dma((2,)), dma((2,)),
            dma((2,)), dma((2,)), dma, dma, dma((4,)), dma((22,)), dma, dma,
            dma, dma((3,)), dma, dma((3,)), dma, dma((3,)), dma, dma((3,)),
        ],
        compiler_params=pltpu.CompilerParams(
            collective_id=0, has_side_effects=True, vmem_limit_bytes=56 * 1024 * 1024
        ),
    )(
        lengths, expert_ids, route_weights, residual, query_latent, norm_gain.reshape(1, D),
        latent_cache.swapaxes(1, 2), w_uv, w_o, w_gate.reshape(D, FF), w_up.reshape(D, FF), w_down.reshape(FF, D),
    )
    return out.reshape(1, D)


def solution(mesh):
    return jax.shard_map(
        on_device,
        mesh=mesh,
        in_specs=(
            P(("dp", "tensor"), None),
            P(("dp", "tensor"), None, None),
            P(("dp", "tensor"), None, None),
            P(("dp", "tensor")),
            P("tensor", None, None),
            P("tensor", "dp", None),
            P(),
            P(("dp", "tensor"), None),
            P(("dp", "tensor"), None),
            P("dp", None, "tensor"),
            P("dp", None, "tensor"),
            P("dp", "tensor", None),
        ),
        out_specs=P(("dp", "tensor"), None),
        check_vma=False,
    )
```
